128 devices in a mesh: blk: 16 (over x, z_lo, core), rep: 8 (over y, z_hi).
Axes of the slice: x: 4, y: 4, z: 4 (z_hi: 2, z_lo: 2; z = z_hi * 2 + z_lo), core: 2. Of those that a mesh axis runs over, the one named last changes fastest.
Arguments:
- features: float32 [49152, 602], P(('blk', 'rep')), may hold values from -6 to 6
- weight: float32 [602, 256], replicated, may hold values from -0.25 to 0.25
- cotangent: float32 [49152, 256], P(('blk', 'rep')), may hold values from -0.10825317 to 0.10825317
- degree: int32 [49152], P(('blk', 'rep')), may hold values from 2 to 13
- tile_row: int32 [16, 8, 256], P('blk', 'rep'), may hold values from 0 to 23, as said below
- tile_col: int32 [16, 8, 256], P('blk', 'rep'), may hold values from 0 to 47
- edge_dst: int32 [16, 8, 256, 256], P('blk', 'rep'), may hold values from 0 to 127
- edge_src: int32 [16, 8, 256, 256], P('blk', 'rep'), may hold values from 0 to 127
- tile_live: int32 [16, 8], P('blk', 'rep'), may hold values from 64 to 256, as said below
Outputs:
- hidden: float32 [49152, 256], P(('blk', 'rep'))
- weight_grad: float32 [602, 256], replicated
The draws below stay inside these ranges and needn't reach their ends.
Inputs may be any that keep to these rules, and one draw needn't show every extreme that they name: On each device the pairs (tile_row, tile_col) of its 256 slots are all different. `tile_live`: at least one device has all 256 slots live.
All inputs are finite; a program needn't handle non-finite values.
Results may differ from the reference program's by a relative error of at most 0.0003.
Values sent between devices are 32-bit elements; how exact they have to be, the bound alone decides.
No kernel may reach another device: no remote copies, remote signals or barrier semaphores. Data moves between devices by JAX's collectives and lax.ppermute only.
A program may use at most 192 MiB of HBM per device.

```python
from functools import partial
import jax
import jax.numpy as jnp
from jax import lax

IN = 602
HID = 256
TILE = 128
BR_DEV = 3
ECAP = 256
TILES_DEV = 256
GROUP_BLOCKS = 24
CYCLE_BLOCKS = 48
NODES = 49152
N_BLK = 16
N_REP = 8


def tile_grid(key):
    key_list = jax.random.split(key, N_BLK * N_REP)
    chosen = jax.vmap(lambda subkey: jax.random.permutation(subkey, GROUP_BLOCKS * CYCLE_BLOCKS)[:TILES_DEV])(key_list)
    return chosen.reshape(N_BLK, N_REP, TILES_DEV).astype(jnp.int32)


def draw_tile_row(key, part):
    return tile_grid(key) // CYCLE_BLOCKS


def draw_tile_col(key, part):
    return tile_grid(key) % CYCLE_BLOCKS


def draw_tile_live(key, part):
    key = jax.random.fold_in(key, 7)
    first_key, second_key = jax.random.split(key)
    counts = jax.random.randint(first_key, (N_BLK * N_REP,), TILES_DEV // 4, TILES_DEV + 1)
    picked = jax.random.randint(second_key, (), 0, N_BLK * N_REP)
    counts = jnp.where(jnp.arange(N_BLK * N_REP) == picked, TILES_DEV, counts)
    return counts.reshape(N_BLK, N_REP).astype(jnp.int32)


def plant(drawn, rng, least, top_value):
    index_at = [jax.random.randint(jax.random.fold_in(rng, axis), (), 0, length) for axis, length in enumerate(drawn.shape)]
    longest = drawn.shape.index(max(drawn.shape))
    neighbour = index_at[:longest] + [(index_at[longest] + 1) % drawn.shape[longest]] + index_at[longest + 1:]
    return drawn.at[tuple(index_at)].set(least).at[tuple(neighbour)].set(top_value)


def shard_levels(stream_key, extent, pieces, least, high):
    def one(position, shards_of):
        steps = jax.random.uniform(jax.random.fold_in(jax.random.fold_in(stream_key, 6), position), (shards_of,), jnp.float32, least / len(pieces), high / len(pieces))
        return jnp.repeat(jnp.exp(steps), extent[position] // shards_of).reshape((-1,) + (1,) * (len(extent) - position - 1))

    level = one(*pieces[0])
    for cut in pieces[1:]:
        level = level * one(*cut)
    return level


def noise(own_key, extent, scale, limit, cuts=(), kind=jnp.bfloat16):
    level = shard_levels(own_key, extent, cuts, -0.22, 0.18) if cuts else 1.0
    values = jax.random.normal(own_key, extent, jnp.float32) * scale * level
    return jnp.minimum(jnp.maximum(values, -limit), limit).astype(kind)


def setup_inputs(seed: int = 0) -> dict:
    key_of = jax.random.split(jax.random.key(seed), 10)
    features = noise(key_of[0], (NODES, IN), 1.0, 6.0, ((0, 128),), jnp.float32)
    weight = noise(key_of[1], (IN, HID), IN ** -0.5, 0.25, (), jnp.float32)
    cotangent = noise(key_of[2], (NODES, HID), (4.0 / NODES ** 0.5), 0.10825317, ((0, 128),), jnp.float32)
    degree = plant(jax.random.randint(key_of[3], (NODES,), 2, 14), jax.random.fold_in(key_of[3], 1), 2, 13).astype(jnp.int32)
    tile_row = draw_tile_row(jax.random.fold_in(key_of[9], 71), 0)
    tile_col = draw_tile_col(jax.random.fold_in(key_of[9], 71), 0)
    edge_dst = plant(jax.random.randint(key_of[6], (N_BLK, N_REP, TILES_DEV, ECAP), 0, TILE), jax.random.fold_in(key_of[6], 1), 0, TILE - 1).astype(jnp.int32)
    edge_src = plant(jax.random.randint(key_of[7], (N_BLK, N_REP, TILES_DEV, ECAP), 0, TILE), jax.random.fold_in(key_of[7], 1), 0, TILE - 1).astype(jnp.int32)
    tile_live = draw_tile_live(jax.random.fold_in(key_of[9], 71), 0)
    return {"features": features, "weight": weight, "cotangent": cotangent, "degree": degree, "tile_row": tile_row, "tile_col": tile_col, "edge_dst": edge_dst, "edge_src": edge_src, "tile_live": tile_live}


HIGH = lax.Precision.HIGHEST
activation = partial(jax.nn.gelu, approximate=True)

def reference(features, weight, cotangent, degree, tile_row, tile_col, edge_dst, edge_src, tile_live):
    scales = lax.rsqrt(degree.astype(features.dtype))[:, None]
    scaled = jnp.dot(features, weight, precision=HIGH, preferred_element_type=jnp.float32) * scales
    blk_ids = jnp.arange(N_BLK, dtype=jnp.int32)[:, None, None]
    rep_ids = jnp.arange(N_REP, dtype=jnp.int32)[None, :, None]
    dst_block = blk_ids * GROUP_BLOCKS + tile_row
    src_block = (tile_col // BR_DEV * N_REP + rep_ids) * BR_DEV + tile_col % BR_DEV
    live_slot = jnp.arange(TILES_DEV, dtype=jnp.int32)[None, None, :] < tile_live[:, :, None]
    dst_node = (dst_block[..., None] * TILE + edge_dst).reshape(N_BLK * N_REP, -1).astype(jnp.int32)
    src_node = (src_block[..., None] * TILE + edge_src).reshape(N_BLK * N_REP, -1).astype(jnp.int32)
    edge_weight = jnp.broadcast_to(live_slot[..., None], edge_dst.shape).reshape(N_BLK * N_REP, -1).astype(features.dtype)

    def spread(values, anchor, target):

        def one_device(totals, item):
            from_ids, to_ids, weights = item
            return (totals.at[to_ids].add(values[from_ids] * weights[:, None]), None)
        totals, unused = lax.scan(one_device, jnp.zeros_like(values), (anchor, target, edge_weight))
        return totals
    forward = spread(scaled, src_node, dst_node)
    pre = (forward + scaled) * scales
    hidden, pull = jax.vjp(activation, pre)
    grad_pre, = pull(cotangent)
    back = grad_pre * scales
    reverse = spread(back, dst_node, src_node)
    grad_rows = (reverse + back) * scales
    weight_grad = jnp.einsum('ni,nh->ih', features, grad_rows, precision=HIGH, preferred_element_type=jnp.float32)
    return (hidden, weight_grad)
```

```python
from functools import partial

import jax
import jax.numpy as jnp
from jax import lax
from jax.experimental import pallas as pl
from jax.experimental.pallas import tpu as pltpu
from jax.sharding import PartitionSpec as P

TILE = 128
HIGH = lax.Precision.HIGHEST
activation = partial(jax.nn.gelu, approximate=True)
CHUNK = 32
UNROLL = 4
VMEM_LIMIT = 60 * 1024 * 1024


def tile_kernel(live_ref, dst_ref, src_ref, out_ref):
    first = pl.program_id(0) * CHUNK
    node_ids = lax.broadcasted_iota(jnp.int32, (TILE, dst_ref.shape[1]), 0)
    for t in range(CHUNK):
        dst_ids = jnp.where(first + t < live_ref[0], dst_ref[t : t + 1, :], TILE)
        dst_hot = (dst_ids == node_ids).astype(jnp.bfloat16)
        src_hot = (src_ref[t : t + 1, :] == node_ids).astype(jnp.bfloat16)
        counts = lax.dot_general(
            dst_hot, src_hot, (((1,), (1,)), ((), ())), preferred_element_type=jnp.float32
        )
        out_ref[t] = counts.astype(jnp.bfloat16)


def build_tiles(live, edge_dst, edge_src):
    slots, edges = edge_dst.shape
    return pl.pallas_call(
        tile_kernel,
        grid_spec=pltpu.PrefetchScalarGridSpec(
            num_scalar_prefetch=1,
            grid=(slots // CHUNK,),
            in_specs=[pl.BlockSpec((CHUNK, edges), lambda g, live: (g, 0))] * 2,
            out_specs=pl.BlockSpec((CHUNK, TILE, TILE), lambda g, live: (g, 0, 0)),
        ),
        out_shape=jax.ShapeDtypeStruct((slots, TILE, TILE), jnp.bfloat16),
        compiler_params=pltpu.CompilerParams(vmem_limit_bytes=VMEM_LIMIT),
        cost_estimate=pl.CostEstimate(
            flops=2 * slots * TILE * TILE * edges, bytes_accessed=10**7, transcendentals=0
        ),
    )(live, edge_dst, edge_src)


def aggregate_kernel(transpose, live_ref, pick_ref, place_ref, tiles_ref, source_ref, out_ref, split):
    step = pl.program_id(0)
    first = step * CHUNK

    @pl.when(step == 0)
    def _():
        out_ref[...] = jnp.zeros_like(out_ref)

        def split_block(b, carry):
            value = source_ref[b]
            high = value.astype(jnp.bfloat16)
            split[b, :TILE] = high
            split[b, TILE:] = (value - high.astype(jnp.float32)).astype(jnp.bfloat16)
            return carry

        lax.fori_loop(0, source_ref.shape[0], split_block, 0)

    left = jnp.clip(live_ref[0] - first, 0, CHUNK)

    def some_tiles(group, carry):
        products = []
        for k in range(UNROLL):
            t = group * UNROLL + k
            tile = tiles_ref[t]
            picked = split[pick_ref[first + t]]
            twice = jnp.concatenate([tile, tile], axis=0 if transpose else 1)
            products.append(
                lax.dot_general(
                    twice,
                    picked,
                    (((0 if transpose else 1,), (0,)), ((), ())),
                    preferred_element_type=jnp.float32,
                )
            )
        for k in range(UNROLL):
            out_ref[place_ref[first + group * UNROLL + k]] += products[k]
        return carry

    lax.fori_loop(0, (left + UNROLL - 1) // UNROLL, some_tiles, 0)


def aggregate(tiles, live, pick_ids, place_ids, source, target_blocks, transpose):
    slots = tiles.shape[0]
    source_blocks, _, width = source.shape
    return pl.pallas_call(
        partial(aggregate_kernel, transpose),
        grid_spec=pltpu.PrefetchScalarGridSpec(
            num_scalar_prefetch=3,
            grid=(slots // CHUNK,),
            in_specs=[
                pl.BlockSpec((CHUNK, TILE, TILE), lambda g, *_: (g, 0, 0)),
                pl.BlockSpec((source_blocks, TILE, width), lambda g, *_: (0, 0, 0)),
            ],
            out_specs=pl.BlockSpec((target_blocks, TILE, width), lambda g, *_: (0, 0, 0)),
            scratch_shapes=[pltpu.VMEM((source_blocks, 2 * TILE, width), jnp.bfloat16)],
        ),
        out_shape=jax.ShapeDtypeStruct((target_blocks, TILE, width), jnp.float32),
        compiler_params=pltpu.CompilerParams(vmem_limit_bytes=VMEM_LIMIT),
        cost_estimate=pl.CostEstimate(
            flops=4 * slots * TILE * TILE * width, bytes_accessed=2 * 10**7, transcendentals=0
        ),
    )(live, pick_ids, place_ids, tiles, source)


def local(features, weight, cotangent, degree, tile_row, tile_col, edge_dst, edge_src, tile_live):
    own_rows = features.shape[0]
    hidden_width = weight.shape[1]
    own_blocks = own_rows // TILE
    group_blocks = own_blocks * lax.axis_size("rep")
    cycle_blocks = own_blocks * lax.axis_size("blk")
    scales = lax.rsqrt(degree.astype(jnp.float32))[:, None]
    row_ids = tile_row.reshape(-1)
    col_ids = tile_col.reshape(-1)
    live = tile_live.reshape(1)
    slots, edges = edge_dst.shape[2:]
    scaled = jnp.dot(features, weight, precision=HIGH, preferred_element_type=jnp.float32) * scales
    cycle_rows = lax.all_gather(scaled, "blk", axis=0, tiled=True)
    tiles = build_tiles(live, edge_dst.reshape(slots, edges), edge_src.reshape(slots, edges))
    sums = aggregate(
        tiles,
        live,
        col_ids,
        row_ids,
        cycle_rows.reshape(cycle_blocks, TILE, hidden_width),
        group_blocks,
        False,
    )
    sums = sums.reshape(group_blocks * TILE, hidden_width)
    own_sums = lax.psum_scatter(sums, "rep", scatter_dimension=0, tiled=True)
    pre = (own_sums + scaled) * scales
    hidden, pull = jax.vjp(activation, pre)
    (own_grad,) = pull(cotangent)
    back_own = own_grad * scales
    back_group = lax.all_gather(back_own, "rep", axis=0, tiled=True)
    reverse = aggregate(
        tiles,
        live,
        row_ids,
        col_ids,
        back_group.reshape(group_blocks, TILE, hidden_width),
        cycle_blocks,
        True,
    )
    reverse = reverse.reshape(cycle_blocks * TILE, hidden_width)
    column_grad = lax.psum_scatter(reverse, "blk", scatter_dimension=0, tiled=True)
    grad_rows = (column_grad + back_own) * scales
    local_grad = jnp.einsum(
        "ni,nh->ih", features, grad_rows, precision=HIGH, preferred_element_type=jnp.float32
    )
    weight_grad = lax.psum(local_grad, ("blk", "rep"))
    return (hidden, weight_grad)


def solution(mesh):
    return jax.shard_map(
        local,
        mesh=mesh,
        in_specs=(
            P(("blk", "rep"), None),
            P(),
            P(("blk", "rep"), None),
            P(("blk", "rep")),
            P("blk", "rep", None),
            P("blk", "rep", None),
            P("blk", "rep", None, None),
            P("blk", "rep", None, None),
            P("blk", "rep"),
        ),
        out_specs=(P(("blk", "rep"), None), P()),
        check_vma=False,
    )
```

```python
from functools import partial

import jax
import jax.numpy as jnp
from jax import lax
from jax.experimental import pallas as pl
from jax.experimental.pallas import tpu as pltpu
from jax.sharding import Mesh
from jax.sharding import PartitionSpec as P

TILE = 128
HIGH = lax.Precision.HIGHEST
activation = partial(jax.nn.gelu, approximate=True)
CHUNK = 32
UNROLL = 4
VMEM_LIMIT = 60 * 1024 * 1024
BLK = ("x", "zl", "core")
REP = ("y", "zh")


def tile_kernel(live_ref, dst_ref, src_ref, out_ref):
    first = pl.program_id(0) * CHUNK
    node_ids = lax.broadcasted_iota(jnp.int32, (TILE, dst_ref.shape[1]), 0)
    for t in range(CHUNK):
        dst_ids = jnp.where(first + t < live_ref[0], dst_ref[t : t + 1, :], TILE)
        dst_hot = (dst_ids == node_ids).astype(jnp.bfloat16)
        src_hot = (src_ref[t : t + 1, :] == node_ids).astype(jnp.bfloat16)
        counts = lax.dot_general(
            dst_hot, src_hot, (((1,), (1,)), ((), ())), preferred_element_type=jnp.float32
        )
        out_ref[t] = counts.astype(jnp.bfloat16)


def build_tiles(live, edge_dst, edge_src):
    slots, edges = edge_dst.shape
    return pl.pallas_call(
        tile_kernel,
        grid_spec=pltpu.PrefetchScalarGridSpec(
            num_scalar_prefetch=1,
            grid=(slots // CHUNK,),
            in_specs=[pl.BlockSpec((CHUNK, edges), lambda g, live: (g, 0))] * 2,
            out_specs=pl.BlockSpec((CHUNK, TILE, TILE), lambda g, live: (g, 0, 0)),
        ),
        out_shape=jax.ShapeDtypeStruct((slots, TILE, TILE), jnp.bfloat16),
        compiler_params=pltpu.CompilerParams(vmem_limit_bytes=VMEM_LIMIT),
        cost_estimate=pl.CostEstimate(
            flops=2 * slots * TILE * TILE * edges, bytes_accessed=10**7, transcendentals=0
        ),
    )(live, edge_dst, edge_src)


def aggregate_kernel(transpose, parts, targets, live_ref, pick_ref, place_ref, tiles_ref, *refs):
    sources, outs = refs[:parts], refs[parts : parts + targets]
    split, totals, sems = refs[parts + targets :]
    step = pl.program_id(0)
    first = step * CHUNK

    @pl.when(step == 0)
    def _():
        totals[...] = jnp.zeros_like(totals)

        for p, source_ref in enumerate(sources):
            count = source_ref.shape[0]

            def split_block(b, carry):
                value = source_ref[b]
                high = value.astype(jnp.bfloat16)
                split[p * count + b, :TILE] = high
                split[p * count + b, TILE:] = (value - high.astype(jnp.float32)).astype(jnp.bfloat16)
                return carry

            lax.fori_loop(0, count, split_block, 0)

    left = jnp.clip(live_ref[0] - first, 0, CHUNK)

    def some_tiles(group, carry):
        products = []
        for k in range(UNROLL):
            t = group * UNROLL + k
            tile = tiles_ref[t]
            picked = split[pick_ref[first + t]]
            twice = jnp.concatenate([tile, tile], axis=0 if transpose else 1)
            products.append(
                lax.dot_general(
                    twice,
                    picked,
                    (((0 if transpose else 1,), (0,)), ((), ())),
                    preferred_element_type=jnp.float32,
                )
            )
        for k in range(UNROLL):
            totals[place_ref[first + group * UNROLL + k]] += products[k]
        return carry

    lax.fori_loop(0, (left + UNROLL - 1) // UNROLL, some_tiles, 0)

    @pl.when(step == pl.num_programs(0) - 1)
    def _():
        copies = []
        for p, out_ref in enumerate(outs):
            count = out_ref.shape[0]
            copy = pltpu.make_async_copy(totals.at[pl.ds(p * count, count)], out_ref, sems.at[p])
            copy.start()
            copies.append(copy)
        for copy in copies:
            copy.wait()


def aggregate(tiles, live, pick_ids, place_ids, sources, target_blocks, transpose):
    slots = tiles.shape[0]
    source_blocks, _, width = sources[0].shape
    parts, targets = len(sources), len(target_blocks)
    return pl.pallas_call(
        partial(aggregate_kernel, transpose, parts, targets),
        grid_spec=pltpu.PrefetchScalarGridSpec(
            num_scalar_prefetch=3,
            grid=(slots // CHUNK,),
            in_specs=[pl.BlockSpec((CHUNK, TILE, TILE), lambda g, *_: (g, 0, 0))]
            + [pl.BlockSpec((source_blocks, TILE, width), lambda g, *_: (0, 0, 0))] * parts,
            out_specs=[pl.BlockSpec(memory_space=pl.ANY)] * targets,
            scratch_shapes=[
                pltpu.VMEM((parts * source_blocks, 2 * TILE, width), jnp.bfloat16),
                pltpu.VMEM((sum(target_blocks), TILE, width), jnp.float32),
                pltpu.SemaphoreType.DMA((targets,)),
            ],
        ),
        out_shape=[jax.ShapeDtypeStruct((b, TILE, width), jnp.float32) for b in target_blocks],
        compiler_params=pltpu.CompilerParams(vmem_limit_bytes=VMEM_LIMIT),
        cost_estimate=pl.CostEstimate(
            flops=4 * slots * TILE * TILE * width, bytes_accessed=2 * 10**7, transcendentals=0
        ),
    )(live, pick_ids, place_ids, tiles, *sources)


def exchange(value, axes):
    return lax.all_to_all(value, axes, 0, 0, tiled=True)


def gather(value, axes):
    return exchange(jnp.broadcast_to(value, (lax.axis_size(axes),) + value.shape), axes)


def swap_cores(value):
    return lax.ppermute(value, "core", [(0, 1), (1, 0)])


def sum_everywhere(value):
    rows, width = value.shape
    parts = lax.axis_size(BLK)
    part_rows = -(-rows // (8 * parts)) * 8
    value = jnp.pad(value, ((0, part_rows * parts - rows), (0, 0)))
    own = exchange(value.reshape(parts, part_rows, width), BLK).sum(0)
    own = gather(own, REP).sum(0)
    return gather(own, BLK).reshape(-1, width)[:rows]


def local(features, weight, cotangent, degree, tile_row, tile_col, edge_dst, edge_src, tile_live):
    own_rows = features.shape[0]
    hidden_width = weight.shape[1]
    own_blocks = own_rows // TILE
    group_blocks = own_blocks * lax.axis_size(REP)
    half_blocks = own_blocks * lax.axis_size(("x", "zl"))
    scales = lax.rsqrt(degree.astype(jnp.float32))[:, None]
    row_ids = tile_row.reshape(-1)
    owner, within = tile_col.reshape(-1) // own_blocks, tile_col.reshape(-1) % own_blocks
    col_ids = (owner % 2 ^ lax.axis_index("core")) * half_blocks + owner // 2 * own_blocks + within
    live = tile_live.reshape(1)
    slots, edges = edge_dst.shape[2:]
    blocks = (-1, TILE, hidden_width)
    scaled = jnp.dot(features, weight, precision=HIGH, preferred_element_type=jnp.float32) * scales
    near = gather(scaled, ("x", "zl"))
    far = swap_cores(near)
    tiles = build_tiles(live, edge_dst.reshape(slots, edges), edge_src.reshape(slots, edges))
    (sums,) = aggregate(
        tiles, live, col_ids, row_ids, [near.reshape(blocks), far.reshape(blocks)], [group_blocks], False
    )
    own_sums = exchange(sums.reshape(-1, own_rows, hidden_width), REP).sum(0)
    pre = (own_sums + scaled) * scales
    hidden, pull = jax.vjp(activation, pre)
    (own_grad,) = pull(cotangent)
    back_own = own_grad * scales
    back_group = gather(back_own, REP)
    near, far = aggregate(
        tiles, live, row_ids, col_ids, [back_group.reshape(blocks)], [half_blocks] * 2, True
    )
    near = near + swap_cores(far)
    column_grad = exchange(near.reshape(-1, own_rows, hidden_width), ("x", "zl")).sum(0)
    grad_rows = (column_grad + back_own) * scales
    local_grad = jnp.einsum(
        "ni,nh->ih", features, grad_rows, precision=HIGH, preferred_element_type=jnp.float32
    )
    return (hidden, sum_everywhere(local_grad))


def solution(mesh):
    mesh = Mesh(mesh.devices.reshape(4, 2, 2, 4, 2), BLK + REP)
    nodes = P(BLK + REP)
    tile = P(BLK, REP)
    return jax.shard_map(
        local,
        mesh=mesh,
        in_specs=(nodes, P(), nodes, nodes, tile, tile, tile, tile, tile),
        out_specs=(nodes, P()),
        check_vma=False,
    )
```

```python
from functools import partial

import jax
import jax.numpy as jnp
from jax import lax
from jax.experimental import pallas as pl
from jax.experimental.pallas import tpu as pltpu
from jax.sharding import Mesh
from jax.sharding import PartitionSpec as P

TILE = 128
HIGH = lax.Precision.HIGHEST
activation = partial(jax.nn.gelu, approximate=True)
ROWS = 8
UNROLL = 4
VMEM_LIMIT = 24 * 1024 * 1024
BLK = ("x", "zl", "core")
REP = ("y", "zh")


def in_vmem(value):
    return pltpu.with_memory_space_constraint(value, pltpu.VMEM)


SMEM = pl.BlockSpec(memory_space=pltpu.SMEM)
VMEM = pl.BlockSpec(memory_space=pltpu.VMEM)


def tile_kernel(live_ref, dst_ref, src_ref, out_ref):
    live = live_ref[0]
    node_ids = lax.broadcasted_iota(jnp.int32, (TILE, dst_ref.shape[1]), 0)

    def some_slots(group, carry):
        first = pl.multiple_of(group * ROWS, ROWS)
        dst = dst_ref[pl.ds(first, ROWS)]
        src = src_ref[pl.ds(first, ROWS)]
        for k in range(ROWS):
            dst_ids = jnp.where(first + k < live, dst[k : k + 1], TILE)
            dst_hot = (dst_ids == node_ids).astype(jnp.bfloat16)
            src_hot = (src[k : k + 1] == node_ids).astype(jnp.bfloat16)
            counts = lax.dot_general(
                dst_hot, src_hot, (((1,), (1,)), ((), ())), preferred_element_type=jnp.float32
            )
            out_ref[first + k] = counts.astype(jnp.bfloat16)
        return carry

    lax.fori_loop(0, (live + ROWS - 1) // ROWS, some_slots, 0)


def build_tiles(live, edge_dst, edge_src):
    slots, edges = edge_dst.shape
    return pl.pallas_call(
        tile_kernel,
        in_specs=[SMEM, VMEM, VMEM],
        out_specs=VMEM,
        out_shape=pltpu.VMEM((slots, TILE, TILE), jnp.bfloat16),
        compiler_params=pltpu.CompilerParams(vmem_limit_bytes=VMEM_LIMIT),
        cost_estimate=pl.CostEstimate(
            flops=2 * slots * TILE * TILE * edges, bytes_accessed=10**7, transcendentals=0
        ),
    )(live, edge_dst, edge_src)


def aggregate_kernel(transpose, parts, live_ref, pick_ref, place_ref, tiles_ref, *refs):
    sources, (start_ref, out_ref, split) = refs[:parts], refs[parts:]
    out_ref[...] = jnp.zeros_like(out_ref)
    if transpose:
        out_ref[: start_ref.shape[0]] = start_ref[...]

    for p, source_ref in enumerate(sources):
        count = source_ref.shape[0]

        def split_block(b, carry):
            value = source_ref[b]
            high = value.astype(jnp.bfloat16)
            split[p * count + b, :TILE] = high
            split[p * count + b, TILE:] = (value - high.astype(jnp.float32)).astype(jnp.bfloat16)
            return carry

        lax.fori_loop(0, count, split_block, 0)

    def some_tiles(group, carry):
        first = group * UNROLL
        products = []
        for k in range(UNROLL):
            tile = tiles_ref[first + k]
            picked = split[pick_ref[first + k]]
            twice = jnp.concatenate([tile, tile], axis=0 if transpose else 1)
            products.append(
                lax.dot_general(
                    twice,
                    picked,
                    (((0 if transpose else 1,), (0,)), ((), ())),
                    preferred_element_type=jnp.float32,
                )
            )
        for k in range(UNROLL):
            out_ref[place_ref[first + k]] += products[k]
        return carry

    lax.fori_loop(0, (live_ref[0] + UNROLL - 1) // UNROLL, some_tiles, 0)


def aggregate(tiles, live, pick_ids, place_ids, sources, start, target_blocks, transpose):
    slots = tiles.shape[0]
    source_blocks, _, width = sources[0].shape
    parts = len(sources)
    return pl.pallas_call(
        partial(aggregate_kernel, transpose, parts),
        in_specs=[SMEM] * 3 + [VMEM] * (parts + 2),
        out_specs=VMEM,
        out_shape=pltpu.VMEM((target_blocks, TILE, width), jnp.float32),
        scratch_shapes=[pltpu.VMEM((parts * source_blocks, 2 * TILE, width), jnp.bfloat16)],
        compiler_params=pltpu.CompilerParams(vmem_limit_bytes=VMEM_LIMIT),
        cost_estimate=pl.CostEstimate(
            flops=4 * slots * TILE * TILE * width, bytes_accessed=2 * 10**7, transcendentals=0
        ),
    )(live, pick_ids, place_ids, in_vmem(tiles), *[in_vmem(v) for v in sources], in_vmem(start))


def gradient_kernel(*refs):
    features, (rows_ref, out_ref) = refs[:-2], refs[-2:]
    two, height, nodes = features[0].shape
    blocks = two * nodes // TILE
    width = out_ref.shape[1]
    piece = height // 2
    out_ref[...] = jnp.zeros_like(out_ref)
    for p, part_ref in enumerate(features):
        rows = rows_ref[p * blocks : (p + 1) * blocks].reshape(blocks * TILE, width)
        rows_high = rows.astype(jnp.bfloat16)
        rows_low = (rows - rows_high.astype(jnp.float32)).astype(jnp.bfloat16)
        right = jnp.concatenate([rows_high, rows_low, rows_high], axis=0)

        def one_piece(m, carry):
            at = pl.ds(pl.multiple_of(m * piece, 16), piece)
            part = jnp.concatenate([part_ref[z, at] for z in range(two)], axis=1)
            high = part.astype(jnp.bfloat16)
            low = (part - high.astype(jnp.float32)).astype(jnp.bfloat16)
            left = jnp.concatenate([high, high, low], axis=1)
            out_ref[at] += jnp.dot(left, right, preferred_element_type=jnp.float32)
            return carry

        lax.fori_loop(0, height // piece, one_piece, 0)


def gradient(features, rows, out_rows):
    width = rows.shape[2]
    return pl.pallas_call(
        gradient_kernel,
        in_specs=[VMEM] * (len(features) + 1),
        out_specs=VMEM,
        out_shape=pltpu.VMEM((out_rows, width), jnp.float32),
        compiler_params=pltpu.CompilerParams(vmem_limit_bytes=VMEM_LIMIT),
        cost_estimate=pl.CostEstimate(
            flops=6 * out_rows * rows.shape[0] * TILE * width, bytes_accessed=10**7, transcendentals=0
        ),
    )(*[in_vmem(f) for f in features], in_vmem(rows))


def exchange(value, axes):
    return lax.all_to_all(value, axes, 0, 0, tiled=True)


def gather(value, axes):
    return exchange(jnp.broadcast_to(value, (lax.axis_size(axes),) + value.shape), axes)


def swap_cores(value):
    return lax.ppermute(value, "core", [(0, 1), (1, 0)])


def sum_everywhere(value):
    rows, width = value.shape
    parts = lax.axis_size(BLK)
    part_rows = -(-rows // (8 * parts)) * 8
    value = jnp.pad(value, ((0, part_rows * parts - rows), (0, 0)))
    own = exchange(value.reshape(parts, part_rows, width), BLK).sum(0)
    own = gather(own, REP).sum(0)
    return gather(own, BLK).reshape(-1, width)[:rows]


def local(features, weight, cotangent, degree, tile_row, tile_col, edge_dst, edge_src, tile_live):
    own_rows, in_width = features.shape
    hidden_width = weight.shape[1]
    own_blocks = own_rows // TILE
    group_blocks = own_blocks * lax.axis_size(REP)
    cycle_blocks = own_blocks * lax.axis_size(BLK)
    blocks = (-1, TILE, hidden_width)
    scales = lax.rsqrt(degree.astype(jnp.float32))[:, None]
    row_ids = tile_row.reshape(-1)
    live = tile_live.reshape(1)
    slots, edges = edge_dst.shape[2:]
    owner, within = tile_col.reshape(-1) // own_blocks, tile_col.reshape(-1) % own_blocks
    other_core = owner % 2 ^ lax.axis_index("core")
    from_ids = other_core * (cycle_blocks // 2) + owner // 2 * own_blocks + within
    x_ahead = (owner // 4 - lax.axis_index("x")) % 4
    other_z = owner // 2 % 2 ^ lax.axis_index("zl")
    to_ids = ((other_core * 4 + x_ahead) * 2 + other_z) * own_blocks + within

    scaled = jnp.dot(features, weight, precision=HIGH, preferred_element_type=jnp.float32) * scales
    near = gather(scaled, ("x", "zl"))
    height = -(-in_width // 32) * 32
    turned = jnp.pad(features.T * scales.T, ((0, height - in_width), (0, 0)))
    turned, near = lax.optimization_barrier((turned, near))
    far = swap_cores(near)
    across = lax.ppermute(turned, "zl", [(0, 1), (1, 0)])
    tiles = build_tiles(live, edge_dst.reshape(slots, edges), edge_src.reshape(slots, edges))
    sums = aggregate(
        tiles, live, from_ids, row_ids, [near.reshape(blocks), far.reshape(blocks)],
        scaled.reshape(blocks), group_blocks, False,
    )
    across, sums = lax.optimization_barrier((across, sums))
    pair = jnp.stack([turned, across])
    cycle = [pair] + [
        lax.ppermute(pair, "x", [(i, (i - ahead) % 4) for i in range(4)]) for ahead in (1, 2, 3)
    ]
    own_sums = exchange(sums.reshape(-1, own_rows, hidden_width), REP).sum(0)
    pre = (own_sums + scaled) * scales
    hidden, pull = jax.vjp(activation, pre)
    (own_grad,) = pull(cotangent)
    back_own = own_grad * scales
    back_group = gather(back_own, REP)
    cycle, back_group = lax.optimization_barrier((cycle, back_group))
    cycle = cycle + [swap_cores(part) for part in cycle]
    reverse = aggregate(
        tiles, live, row_ids, to_ids, [back_group.reshape(blocks)],
        back_own.reshape(blocks), cycle_blocks, True,
    )
    cycle, reverse = lax.optimization_barrier((cycle, reverse))
    parts = lax.axis_size(BLK)
    out_rows = -(-in_width // (8 * parts)) * 8 * parts
    return (hidden, sum_everywhere(gradient(cycle, reverse, out_rows))[:in_width])


def solution(mesh):
    mesh = Mesh(mesh.devices.reshape(4, 2, 2, 4, 2), BLK + REP)
    nodes = P(BLK + REP)
    tile = P(BLK, REP)
    return jax.shard_map(
        local,
        mesh=mesh,
        in_specs=(nodes, P(), nodes, nodes, tile, tile, tile, tile, tile),
        out_specs=(nodes, P()),
        check_vma=False,
    )
```

```python
from functools import partial

import jax
import jax.numpy as jnp
from jax import lax
from jax.experimental import pallas as pl
from jax.experimental.pallas import tpu as pltpu
from jax.sharding import Mesh
from jax.sharding import PartitionSpec as P

TILE = 128
HIGH = lax.Precision.HIGHEST
activation = partial(jax.nn.gelu, approximate=True)
ROWS = 32
PIECE = 6
UNROLL = 32
VMEM_LIMIT = 24 * 1024 * 1024
BLK = ("x", "zl", "core")
REP = ("y", "zh")


def in_vmem(value):
    return pltpu.with_memory_space_constraint(value, pltpu.VMEM)


SMEM = pl.BlockSpec(memory_space=pltpu.SMEM)
VMEM = pl.BlockSpec(memory_space=pltpu.VMEM)


def tile_kernel(live_ref, dst_ref, src_ref, out_ref):
    live = live_ref[0]
    node_ids = lax.broadcasted_iota(jnp.int32, (TILE, dst_ref.shape[1]), 0)

    def some_slots(group, carry):
        first = pl.multiple_of(group * ROWS, ROWS)
        dst = dst_ref[pl.ds(first, ROWS)]
        src = src_ref[pl.ds(first, ROWS)]
        for k in range(ROWS):
            dst_ids = jnp.where(first + k < live, dst[k : k + 1], TILE)
            dst_hot = (dst_ids == node_ids).astype(jnp.bfloat16)
            src_hot = (src[k : k + 1] == node_ids).astype(jnp.bfloat16)
            counts = lax.dot_general(
                dst_hot, src_hot, (((1,), (1,)), ((), ())), preferred_element_type=jnp.float32
            )
            out_ref[first + k] = counts.astype(jnp.bfloat16)
        return carry

    lax.fori_loop(0, (live + ROWS - 1) // ROWS, some_slots, 0)


def build_tiles(live, edge_dst, edge_src):
    slots, edges = edge_dst.shape
    return pl.pallas_call(
        tile_kernel,
        in_specs=[SMEM, VMEM, VMEM],
        out_specs=VMEM,
        out_shape=pltpu.VMEM((slots, TILE, TILE), jnp.bfloat16),
        compiler_params=pltpu.CompilerParams(vmem_limit_bytes=VMEM_LIMIT),
        cost_estimate=pl.CostEstimate(
            flops=2 * slots * TILE * TILE * edges, bytes_accessed=10**7, transcendentals=0
        ),
    )(live, edge_dst, edge_src)


def aggregate_kernel(transpose, parts, targets, live_ref, pick_ref, place_ref, tiles_ref, *refs):
    sources, outs, (split, totals, landed, sems) = (
        refs[:parts],
        refs[parts : parts + targets],
        refs[parts + targets :],
    )
    pieces = [
        (p, b) for p, source_ref in enumerate(sources) for b in range(0, source_ref.shape[0], PIECE)
    ]
    copies = []
    for n, (p, b) in enumerate(pieces):
        copy = pltpu.make_async_copy(
            sources[p].at[pl.ds(b, PIECE)], landed.at[pl.ds(n * PIECE, PIECE)], sems.at[n]
        )
        copy.start()
        copies.append(copy)
    totals[...] = jnp.zeros_like(totals)

    for n, copy in enumerate(copies):
        copy.wait()

        def split_block(k, carry):
            value = landed[n * PIECE + k]
            high = value.astype(jnp.bfloat16)
            split[n * PIECE + k, :TILE] = high
            split[n * PIECE + k, TILE:] = (value - high.astype(jnp.float32)).astype(jnp.bfloat16)
            return carry

        lax.fori_loop(0, PIECE, split_block, 0)

    def some_tiles(group, carry):
        first = group * UNROLL
        products = []
        for k in range(UNROLL):
            tile = tiles_ref[first + k]
            picked = split[pick_ref[first + k]]
            twice = jnp.concatenate([tile, tile], axis=0 if transpose else 1)
            products.append(
                lax.dot_general(
                    twice,
                    picked,
                    (((0 if transpose else 1,), (0,)), ((), ())),
                    preferred_element_type=jnp.float32,
                )
            )
        for k in range(UNROLL):
            totals[place_ref[first + k]] += products[k]
        return carry

    lax.fori_loop(0, (live_ref[0] + UNROLL - 1) // UNROLL, some_tiles, 0)
    for p, out_ref in enumerate(outs):
        count = out_ref.shape[0]
        out_ref[...] = totals[p * count : (p + 1) * count]


def aggregate(tiles, live, pick_ids, place_ids, sources, target_blocks, transpose):
    slots = tiles.shape[0]
    source_blocks, _, width = sources[0].shape
    parts, targets = len(sources), len(target_blocks)
    return pl.pallas_call(
        partial(aggregate_kernel, transpose, parts, targets),
        in_specs=[SMEM] * 3 + [VMEM] + [pl.BlockSpec(memory_space=pl.ANY)] * parts,
        out_specs=[VMEM] * targets,
        out_shape=[pltpu.VMEM((b, TILE, width), jnp.float32) for b in target_blocks],
        scratch_shapes=[
            pltpu.VMEM((parts * source_blocks, 2 * TILE, width), jnp.bfloat16),
            pltpu.VMEM((sum(target_blocks), TILE, width), jnp.float32),
            pltpu.VMEM((parts * source_blocks, TILE, width), jnp.float32),
            pltpu.SemaphoreType.DMA((parts * source_blocks // PIECE,)),
        ],
        compiler_params=pltpu.CompilerParams(vmem_limit_bytes=VMEM_LIMIT),
        cost_estimate=pl.CostEstimate(
            flops=4 * slots * TILE * TILE * width, bytes_accessed=2 * 10**7, transcendentals=0
        ),
    )(live, pick_ids, place_ids, in_vmem(tiles), *sources)


def exchange(value, axes):
    return lax.all_to_all(value, axes, 0, 0, tiled=True)


def gather(value, axes):
    return exchange(jnp.broadcast_to(value, (lax.axis_size(axes),) + value.shape), axes)


def swap_cores(value):
    return lax.ppermute(value, "core", [(0, 1), (1, 0)])


def sum_everywhere(value):
    rows, width = value.shape
    parts = lax.axis_size(BLK)
    part_rows = -(-rows // (8 * parts)) * 8
    value = jnp.pad(value, ((0, part_rows * parts - rows), (0, 0)))
    own = exchange(value.reshape(parts, part_rows, width), BLK).sum(0)
    own = gather(own, REP).sum(0)
    return gather(own, BLK).reshape(-1, width)[:rows]


def local(features, weight, cotangent, degree, tile_row, tile_col, edge_dst, edge_src, tile_live):
    own_rows = features.shape[0]
    hidden_width = weight.shape[1]
    own_blocks = own_rows // TILE
    group_blocks = own_blocks * lax.axis_size(REP)
    half_blocks = own_blocks * lax.axis_size(("x", "zl"))
    scales = lax.rsqrt(degree.astype(jnp.float32))[:, None]
    row_ids = tile_row.reshape(-1)
    owner, within = tile_col.reshape(-1) // own_blocks, tile_col.reshape(-1) % own_blocks
    col_ids = (owner % 2 ^ lax.axis_index("core")) * half_blocks + owner // 2 * own_blocks + within
    live = tile_live.reshape(1)
    slots, edges = edge_dst.shape[2:]
    blocks = (-1, TILE, hidden_width)
    scaled = jnp.dot(features, weight, precision=HIGH, preferred_element_type=jnp.float32) * scales
    near = gather(scaled, ("x", "zl"))
    far = swap_cores(near)
    tiles = build_tiles(live, edge_dst.reshape(slots, edges), edge_src.reshape(slots, edges))
    (sums,) = aggregate(
        tiles, live, col_ids, row_ids, [near.reshape(blocks), far.reshape(blocks)], [group_blocks], False
    )
    own_sums = exchange(sums.reshape(-1, own_rows, hidden_width), REP).sum(0)
    pre = (own_sums + scaled) * scales
    hidden, pull = jax.vjp(activation, pre)
    (own_grad,) = pull(cotangent)
    back_own = own_grad * scales
    back_group = gather(back_own, REP)
    near, far = aggregate(
        tiles, live, row_ids, col_ids, [back_group.reshape(blocks)], [half_blocks] * 2, True
    )
    near = near + swap_cores(far)
    column_grad = exchange(near.reshape(-1, own_rows, hidden_width), ("x", "zl")).sum(0)
    grad_rows = (column_grad + back_own) * scales
    local_grad = jnp.einsum(
        "ni,nh->ih", features, grad_rows, precision=HIGH, preferred_element_type=jnp.float32
    )
    return (hidden, sum_everywhere(local_grad))


def solution(mesh):
    mesh = Mesh(mesh.devices.reshape(4, 2, 2, 4, 2), BLK + REP)
    nodes = P(BLK + REP)
    tile = P(BLK, REP)
    return jax.shard_map(
        local,
        mesh=mesh,
        in_specs=(nodes, P(), nodes, nodes, tile, tile, tile, tile, tile),
        out_specs=(nodes, P()),
        check_vma=False,
    )
```

```python
from functools import partial

import jax
import jax.numpy as jnp
from jax import lax
from jax.experimental import pallas as pl
from jax.experimental.pallas import tpu as pltpu
from jax.sharding import Mesh
from jax.sharding import PartitionSpec as P

TILE = 128
HIGH = lax.Precision.HIGHEST
activation = partial(jax.nn.gelu, approximate=True)
ROWS = 32
PIECE = 6
PARTS = 2
UNROLL = 32
VMEM_LIMIT = 32 * 1024 * 1024
BLK = ("x", "zl", "core")
REP = ("y", "zh")


def in_vmem(value):
    return pltpu.with_memory_space_constraint(value, pltpu.VMEM)


def in_hbm(value):
    return pltpu.with_memory_space_constraint(value, pltpu.HBM)


SMEM = pl.BlockSpec(memory_space=pltpu.SMEM)
VMEM = pl.BlockSpec(memory_space=pltpu.VMEM)
ANY = pl.BlockSpec(memory_space=pl.ANY)


def tile_kernel(live_ref, dst_hbm, src_hbm, out_ref, dst_ref, src_ref, tiles, edge_sems, sems):
    live = live_ref[0]
    groups = (live + ROWS - 1) // ROWS
    node_ids = lax.broadcasted_iota(jnp.int32, (TILE, dst_ref.shape[1]), 0)

    def copies_in(group):
        at = pl.ds(pl.multiple_of(group * ROWS, ROWS), ROWS)
        return [
            pltpu.make_async_copy(dst_hbm.at[at], dst_ref.at[at], edge_sems.at[0, group]),
            pltpu.make_async_copy(src_hbm.at[at], src_ref.at[at], edge_sems.at[1, group]),
        ]

    def start_in(group, carry):
        for copy in copies_in(group):
            copy.start()
        return carry

    def copy_out(group):
        at = pl.ds(pl.multiple_of(group * ROWS, ROWS), ROWS)
        return pltpu.make_async_copy(tiles.at[at], out_ref.at[at], sems.at[group])

    def some_slots(group, carry):
        for copy in copies_in(group):
            copy.wait()
        first = pl.multiple_of(group * ROWS, ROWS)
        dst = dst_ref[pl.ds(first, ROWS)]
        src = src_ref[pl.ds(first, ROWS)]
        for k in range(ROWS):
            dst_ids = jnp.where(first + k < live, dst[k : k + 1], TILE)
            dst_hot = (dst_ids == node_ids).astype(jnp.bfloat16)
            src_hot = (src[k : k + 1] == node_ids).astype(jnp.bfloat16)
            counts = lax.dot_general(
                dst_hot, src_hot, (((1,), (1,)), ((), ())), preferred_element_type=jnp.float32
            )
            tiles[first + k] = counts.astype(jnp.bfloat16)
        copy_out(group).start()
        return carry

    lax.fori_loop(0, groups, start_in, 0)
    lax.fori_loop(0, groups, some_slots, 0)
    lax.fori_loop(0, groups, lambda group, carry: (copy_out(group).wait(), carry)[1], 0)


def build_tiles(live, edge_dst, edge_src):
    slots, edges = edge_dst.shape
    return pl.pallas_call(
        tile_kernel,
        in_specs=[SMEM, ANY, ANY],
        out_specs=ANY,
        out_shape=pltpu.HBM((slots, TILE, TILE), jnp.bfloat16),
        scratch_shapes=[
            pltpu.VMEM((slots, edges), jnp.int32),
            pltpu.VMEM((slots, edges), jnp.int32),
            pltpu.VMEM((slots, TILE, TILE), jnp.bfloat16),
            pltpu.SemaphoreType.DMA((2, slots // ROWS)),
            pltpu.SemaphoreType.DMA((slots // ROWS,)),
        ],
        compiler_params=pltpu.CompilerParams(vmem_limit_bytes=VMEM_LIMIT),
        cost_estimate=pl.CostEstimate(flops=10**6, bytes_accessed=10**5, transcendentals=0),
    )(live, in_hbm(edge_dst), in_hbm(edge_src))


def aggregate_kernel(transpose, parts, targets, live_ref, pick_ref, place_ref, tiles_ref, *refs):
    sources, outs = refs[:parts], refs[parts : parts + targets]
    split, totals, landed, tiles, sems, tile_sems = refs[parts + targets :]
    groups = (live_ref[0] + UNROLL - 1) // UNROLL

    def tile_copy(group):
        at = pl.ds(pl.multiple_of(group * UNROLL, UNROLL), UNROLL)
        return pltpu.make_async_copy(tiles_ref.at[at], tiles.at[at], tile_sems.at[group])

    pieces = [
        (p, b) for p, source_ref in enumerate(sources) for b in range(0, source_ref.shape[0], PIECE)
    ]
    copies = []
    for n, (p, b) in enumerate(pieces):
        copy = pltpu.make_async_copy(
            sources[p].at[pl.ds(b, PIECE)], landed.at[pl.ds(n * PIECE, PIECE)], sems.at[n]
        )
        copy.start()
        copies.append(copy)
    lax.fori_loop(0, groups, lambda group, carry: (tile_copy(group).start(), carry)[1], 0)
    totals[...] = jnp.zeros_like(totals)

    for n, copy in enumerate(copies):
        copy.wait()

        def split_block(k, carry):
            value = landed[n * PIECE + k]
            high = value.astype(jnp.bfloat16)
            split[n * PIECE + k, :TILE] = high
            split[n * PIECE + k, TILE:] = (value - high.astype(jnp.float32)).astype(jnp.bfloat16)
            return carry

        lax.fori_loop(0, PIECE, split_block, 0)

    def some_tiles(group, carry):
        tile_copy(group).wait()
        first = group * UNROLL
        products = []
        for k in range(UNROLL):
            tile = tiles[first + k]
            picked = split[pick_ref[first + k]]
            twice = jnp.concatenate([tile, tile], axis=0 if transpose else 1)
            products.append(
                lax.dot_general(
                    twice,
                    picked,
                    (((0 if transpose else 1,), (0,)), ((), ())),
                    preferred_element_type=jnp.float32,
                )
            )
        for k in range(UNROLL):
            totals[place_ref[first + k]] += products[k]
        return carry

    lax.fori_loop(0, groups, some_tiles, 0)
    for p, out_ref in enumerate(outs):
        count = out_ref.shape[0]
        out_ref[...] = totals[p * count : (p + 1) * count]


def aggregate(tiles, live, pick_ids, place_ids, sources, target_blocks, transpose):
    slots = tiles.shape[0]
    source_blocks, _, width = sources[0].shape
    parts, targets = len(sources), len(target_blocks)
    return pl.pallas_call(
        partial(aggregate_kernel, transpose, parts, targets),
        in_specs=[SMEM] * 3 + [ANY] * (1 + parts),
        out_specs=[VMEM] * targets,
        out_shape=[pltpu.VMEM((b, TILE, width), jnp.float32) for b in target_blocks],
        scratch_shapes=[
            pltpu.VMEM((parts * source_blocks, 2 * TILE, width), jnp.bfloat16),
            pltpu.VMEM((sum(target_blocks), TILE, width), jnp.float32),
            pltpu.VMEM((parts * source_blocks, TILE, width), jnp.float32),
            pltpu.VMEM(tiles.shape, jnp.bfloat16),
            pltpu.SemaphoreType.DMA((parts * source_blocks // PIECE,)),
            pltpu.SemaphoreType.DMA((slots // UNROLL,)),
        ],
        compiler_params=pltpu.CompilerParams(vmem_limit_bytes=VMEM_LIMIT),
        cost_estimate=pl.CostEstimate(
            flops=10**6, bytes_accessed=10**5, transcendentals=0
        ),
    )(live, pick_ids, place_ids, in_hbm(tiles), *sources)


def gradient_kernel(*refs):
    features, (rows_ref, out_ref) = refs[:-2], refs[-2:]
    height, nodes = features[0].shape
    blocks = PARTS * nodes // TILE
    width = out_ref.shape[1]
    out_ref[...] = jnp.zeros_like(out_ref)
    for p in range(0, len(features), PARTS):
        part = jnp.concatenate([f[...] for f in features[p : p + PARTS]], axis=1)
        first = p * nodes // TILE
        rows = rows_ref[first : first + blocks].reshape(blocks * TILE, width)
        rows_high = rows.astype(jnp.bfloat16)
        rows_low = (rows - rows_high.astype(jnp.float32)).astype(jnp.bfloat16)
        right = jnp.concatenate([rows_high, rows_low, rows_high], axis=0)
        high = part.astype(jnp.bfloat16)
        low = (part - high.astype(jnp.float32)).astype(jnp.bfloat16)
        left = jnp.concatenate([high, high, low], axis=1)
        out_ref[:height] += jnp.dot(left, right, preferred_element_type=jnp.float32)


def gradient(features, rows, out_rows):
    width = rows.shape[2]
    return pl.pallas_call(
        gradient_kernel,
        in_specs=[VMEM] * (len(features) + 1),
        out_specs=VMEM,
        out_shape=pltpu.VMEM((out_rows, width), jnp.float32),
        compiler_params=pltpu.CompilerParams(vmem_limit_bytes=VMEM_LIMIT),
        cost_estimate=pl.CostEstimate(
            flops=6 * out_rows * rows.shape[0] * TILE * width, bytes_accessed=10**7, transcendentals=0
        ),
    )(*[in_vmem(f) for f in features], in_vmem(rows))


def exchange(value, axes):
    return lax.all_to_all(value, axes, 0, 0, tiled=True)


def gather(value, axes):
    return exchange(jnp.broadcast_to(value, (lax.axis_size(axes),) + value.shape), axes)


def swap(value, axis):
    return lax.ppermute(value, axis, [(0, 1), (1, 0)])


def from_ahead(value, axis, steps):
    size = lax.axis_size(axis)
    return lax.ppermute(value, axis, [(i, (i - steps) % size) for i in range(size)])


def sum_everywhere(value):
    rows, width = value.shape
    parts = lax.axis_size(BLK)
    part_rows = -(-rows // (8 * parts)) * 8
    value = jnp.pad(value, ((0, part_rows * parts - rows), (0, 0)))
    own = exchange(value.reshape(parts, part_rows, width), BLK).sum(0)
    own = gather(own, REP).sum(0)
    return gather(own, BLK).reshape(-1, width)[:rows]


def local(features, weight, cotangent, degree, tile_row, tile_col, edge_dst, edge_src, tile_live):
    own_rows, in_width = features.shape
    hidden_width = weight.shape[1]
    own_blocks = own_rows // TILE
    group_blocks = own_blocks * lax.axis_size(REP)
    half_blocks = own_blocks * lax.axis_size(("x", "zl"))
    blocks = (-1, TILE, hidden_width)
    scales = lax.rsqrt(degree.astype(jnp.float32))[:, None]
    row_ids = tile_row.reshape(-1)
    live = tile_live.reshape(1)
    slots, edges = edge_dst.shape[2:]
    owner, within = tile_col.reshape(-1) // own_blocks, tile_col.reshape(-1) % own_blocks
    other_core = owner % 2 ^ lax.axis_index("core")
    from_ids = other_core * half_blocks + owner // 2 * own_blocks + within
    x_ahead = (owner // 4 - lax.axis_index("x")) % 4
    other_z = owner // 2 % 2 ^ lax.axis_index("zl")
    to_ids = other_core * half_blocks + (x_ahead * 2 + other_z) * own_blocks + within

    scaled = jnp.dot(features, weight, precision=HIGH, preferred_element_type=jnp.float32) * scales
    height = -(-in_width // 32) * 32
    here = jnp.pad(features.T * scales.T, ((0, height - in_width), (0, 0)))
    scaled, here = lax.optimization_barrier((scaled, here))
    near = gather(scaled, ("x", "zl"))
    here, near = lax.optimization_barrier((here, near))
    far = swap(near, "core")
    across = swap(here, "zl")
    here_x = [from_ahead(here, "x", steps) for steps in (1, 2, 3)]
    tiles = build_tiles(live, edge_dst.reshape(slots, edges), edge_src.reshape(slots, edges))

    def forward(near, far, scaled, cotangent):
        sources = [near.reshape(blocks), far.reshape(blocks)]
        (sums,) = aggregate(tiles, live, from_ids, row_ids, sources, [group_blocks], False)
        own_sums = exchange(sums.reshape(-1, own_rows, hidden_width), REP).sum(0)
        hidden, pull = jax.vjp(activation, (own_sums + scaled) * scales)
        return hidden, pull(cotangent)[0] * scales

    def never(near, far, scaled, cotangent):
        return scaled + cotangent, scaled - cotangent

    hidden, back_own = lax.cond(live[0] > 0, forward, never, near, far, scaled, cotangent)
    across, here_x, back_own = lax.optimization_barrier((across, here_x, back_own))
    across_x = [from_ahead(across, "x", steps) for steps in (1, 2, 3)]
    back_group = lax.cond(
        live[0] > 0,
        lambda back: gather(back, REP),
        lambda back: jnp.broadcast_to(back, (lax.axis_size(REP),) + back.shape),
        back_own,
    )
    across_x, back_group = lax.optimization_barrier((across_x, back_group))
    kept, sent = aggregate(
        tiles, live, row_ids, to_ids, [back_group.reshape(blocks)], [half_blocks] * 2, True
    )
    kept = kept + swap(sent, "core")
    kept = kept + jnp.pad(back_own.reshape(blocks), ((0, half_blocks - own_blocks), (0, 0), (0, 0)))
    held = [part for pair in zip([here, *here_x], [across, *across_x]) for part in pair]
    parts = lax.axis_size(BLK)
    out_rows = -(-in_width // (8 * parts)) * 8 * parts
    return (hidden, sum_everywhere(gradient(held, kept, out_rows))[:in_width])


def solution(mesh):
    mesh = Mesh(mesh.devices.reshape(4, 2, 2, 4, 2), BLK + REP)
    nodes = P(BLK + REP)
    tile = P(BLK, REP)
    return jax.shard_map(
        local,
        mesh=mesh,
        in_specs=(nodes, P(), nodes, nodes, tile, tile, tile, tile, tile),
        out_specs=(nodes, P()),
        check_vma=False,
    )
```

```python
from functools import partial

import jax
import jax.numpy as jnp
from jax import lax
from jax.experimental import pallas as pl
from jax.experimental.pallas import tpu as pltpu
from jax.sharding import Mesh
from jax.sharding import PartitionSpec as P

TILE = 128
HIGH = lax.Precision.HIGHEST
activation = partial(jax.nn.gelu, approximate=True)
ROWS = 32
PIECE = 6
PARTS = 2
STRIP = 128
UNROLL = 32
VMEM_LIMIT = 32 * 1024 * 1024
BLK = ("x", "zl", "core")
REP = ("y", "zh")


def in_vmem(value):
    return pltpu.with_memory_space_constraint(value, pltpu.VMEM)


def in_hbm(value):
    return pltpu.with_memory_space_constraint(value, pltpu.HBM)


SMEM = pl.BlockSpec(memory_space=pltpu.SMEM)
VMEM = pl.BlockSpec(memory_space=pltpu.VMEM)
ANY = pl.BlockSpec(memory_space=pl.ANY)


def tile_kernel(live_ref, dst_hbm, src_hbm, out_ref, dst_ref, src_ref, tiles, edge_sems, sems):
    live = live_ref[0]
    groups = (live + ROWS - 1) // ROWS
    node_ids = lax.broadcasted_iota(jnp.int32, (TILE, dst_ref.shape[1]), 0).astype(jnp.float32).astype(jnp.bfloat16)
    one, zero = jnp.ones((), jnp.bfloat16), jnp.zeros((), jnp.bfloat16)

    def one_hot(ids):
        return jnp.where(ids.astype(jnp.float32).astype(jnp.bfloat16) == node_ids, one, zero)

    def copies_in(group):
        at = pl.ds(pl.multiple_of(group * ROWS, ROWS), ROWS)
        return [
            pltpu.make_async_copy(dst_hbm.at[at], dst_ref.at[at], edge_sems.at[0, group]),
            pltpu.make_async_copy(src_hbm.at[at], src_ref.at[at], edge_sems.at[1, group]),
        ]

    def start_in(group, carry):
        for copy in copies_in(group):
            copy.start()
        return carry

    def copy_out(group):
        at = pl.ds(pl.multiple_of(group * ROWS, ROWS), ROWS)
        return pltpu.make_async_copy(tiles.at[at], out_ref.at[at], sems.at[group])

    def some_slots(group, carry):
        for copy in copies_in(group):
            copy.wait()
        first = pl.multiple_of(group * ROWS, ROWS)
        dst = dst_ref[pl.ds(first, ROWS)]
        src = src_ref[pl.ds(first, ROWS)]
        for k in range(ROWS):
            dst_ids = jnp.where(first + k < live, dst[k : k + 1], TILE)
            counts = lax.dot_general(
                one_hot(dst_ids),
                one_hot(src[k : k + 1]),
                (((1,), (1,)), ((), ())),
                preferred_element_type=jnp.float32,
            )
            tiles[first + k] = counts.astype(jnp.bfloat16)
        copy_out(group).start()
        return carry

    lax.fori_loop(0, groups, start_in, 0)
    lax.fori_loop(0, groups, some_slots, 0)
    lax.fori_loop(0, groups, lambda group, carry: (copy_out(group).wait(), carry)[1], 0)


def build_tiles(live, edge_dst, edge_src):
    slots, edges = edge_dst.shape
    return pl.pallas_call(
        tile_kernel,
        in_specs=[SMEM, ANY, ANY],
        out_specs=ANY,
        out_shape=pltpu.HBM((slots, TILE, TILE), jnp.bfloat16),
        scratch_shapes=[
            pltpu.VMEM((slots, edges), jnp.int32),
            pltpu.VMEM((slots, edges), jnp.int32),
            pltpu.VMEM((slots, TILE, TILE), jnp.bfloat16),
            pltpu.SemaphoreType.DMA((2, slots // ROWS)),
            pltpu.SemaphoreType.DMA((slots // ROWS,)),
        ],
        compiler_params=pltpu.CompilerParams(vmem_limit_bytes=VMEM_LIMIT),
        cost_estimate=pl.CostEstimate(flops=10**6, bytes_accessed=10**5, transcendentals=0),
    )(live, in_hbm(edge_dst), in_hbm(edge_src))


def aggregate_kernel(transpose, parts, targets, live_ref, pick_ref, place_ref, tiles_ref, *refs):
    sources, outs = refs[:parts], refs[parts : parts + targets]
    split, landed, tiles, sems, tile_sems, *more = refs[parts + targets :]
    totals = more[0] if more else outs[0]
    groups = (live_ref[0] + UNROLL - 1) // UNROLL

    def tile_copy(group):
        at = pl.ds(pl.multiple_of(group * UNROLL, UNROLL), UNROLL)
        return pltpu.make_async_copy(tiles_ref.at[at], tiles.at[at], tile_sems.at[group])

    pieces = [
        (p, b) for p, source_ref in enumerate(sources) for b in range(0, source_ref.shape[0], PIECE)
    ]
    copies = []
    for n, (p, b) in enumerate(pieces):
        copy = pltpu.make_async_copy(
            sources[p].at[pl.ds(b, PIECE)], landed.at[pl.ds(n * PIECE, PIECE)], sems.at[n]
        )
        copy.start()
        copies.append(copy)
    lax.fori_loop(0, groups, lambda group, carry: (tile_copy(group).start(), carry)[1], 0)
    totals[...] = jnp.zeros_like(totals)

    for n, copy in enumerate(copies):
        copy.wait()

        def split_block(k, carry):
            value = landed[n * PIECE + k]
            high = value.astype(jnp.bfloat16)
            split[n * PIECE + k, :TILE] = high
            split[n * PIECE + k, TILE:] = (value - high.astype(jnp.float32)).astype(jnp.bfloat16)
            return carry

        lax.fori_loop(0, PIECE, split_block, 0)

    def some_tiles(group, carry):
        tile_copy(group).wait()
        first = group * UNROLL
        products = []
        for k in range(UNROLL):
            tile = tiles[first + k]
            picked = split[pick_ref[first + k]]
            twice = jnp.concatenate([tile, tile], axis=0 if transpose else 1)
            products.append(
                lax.dot_general(
                    twice,
                    picked,
                    (((0 if transpose else 1,), (0,)), ((), ())),
                    preferred_element_type=jnp.float32,
                )
            )
        for k in range(UNROLL):
            totals[place_ref[first + k]] += products[k]
        return carry

    lax.fori_loop(0, groups, some_tiles, 0)
    if more:
        for p, out_ref in enumerate(outs):
            count = out_ref.shape[0]
            out_ref[...] = totals[p * count : (p + 1) * count]


def aggregate(tiles, live, pick_ids, place_ids, sources, target_blocks, transpose):
    slots = tiles.shape[0]
    source_blocks, _, width = sources[0].shape
    parts, targets = len(sources), len(target_blocks)
    return pl.pallas_call(
        partial(aggregate_kernel, transpose, parts, targets),
        in_specs=[SMEM] * 3 + [ANY] * (1 + parts),
        out_specs=[VMEM] * targets,
        out_shape=[pltpu.VMEM((b, TILE, width), jnp.float32) for b in target_blocks],
        scratch_shapes=[
            pltpu.VMEM((parts * source_blocks, 2 * TILE, width), jnp.bfloat16),
            pltpu.VMEM((parts * source_blocks, TILE, width), jnp.float32),
            pltpu.VMEM(tiles.shape, jnp.bfloat16),
            pltpu.SemaphoreType.DMA((parts * source_blocks // PIECE,)),
            pltpu.SemaphoreType.DMA((slots // UNROLL,)),
        ]
        + [pltpu.VMEM((sum(target_blocks), TILE, width), jnp.float32)] * (targets > 1),
        compiler_params=pltpu.CompilerParams(vmem_limit_bytes=VMEM_LIMIT),
        cost_estimate=pl.CostEstimate(
            flops=10**6, bytes_accessed=10**5, transcendentals=0
        ),
    )(live, pick_ids, place_ids, in_hbm(tiles), *sources)


def activate_kernel(parts_ref, scaled_ref, cotangent_ref, scales_ref, hidden_ref, back_ref):
    scales = jnp.concatenate([scales_ref[...]] * (hidden_ref.shape[1] // TILE), axis=1)
    pre = (parts_ref[...].sum(0) + scaled_ref[...]) * scales
    hidden, pull = jax.vjp(activation, pre)
    hidden_ref[...] = hidden
    back_ref[...] = pull(cotangent_ref[...])[0] * scales


def activate(parts, scaled, cotangent, scales):
    count, rows, width = parts.shape
    block = pl.BlockSpec((STRIP, width), lambda g: (g, 0))
    return pl.pallas_call(
        activate_kernel,
        grid=(rows // STRIP,),
        in_specs=[
            pl.BlockSpec((count, STRIP, width), lambda g: (0, g, 0)),
            block,
            block,
            pl.BlockSpec((STRIP, TILE), lambda g: (g, 0)),
        ],
        out_specs=[block, block],
        out_shape=[jax.ShapeDtypeStruct((rows, width), jnp.float32)] * 2,
        compiler_params=pltpu.CompilerParams(vmem_limit_bytes=VMEM_LIMIT),
    )(parts, scaled, cotangent, scales)


def gradient_kernel(*refs):
    features, (core_ref, rows_ref, mine_ref, other_ref, out_ref) = refs[:-5], refs[-5:]
    height, nodes = features[0].shape
    blocks = PARTS * nodes // TILE
    width = out_ref.shape[1]
    out_ref[...] = jnp.zeros_like(out_ref)
    for p in range(0, len(features), PARTS):
        part = jnp.concatenate([f[...] for f in features[p : p + PARTS]], axis=1)
        first = p * nodes // TILE
        rows = rows_ref[first : first + blocks].reshape(blocks * TILE, width)
        rows_high = rows.astype(jnp.bfloat16)
        rows_low = (rows - rows_high.astype(jnp.float32)).astype(jnp.bfloat16)
        right = jnp.concatenate([rows_high, rows_low, rows_high], axis=0)
        high = part.astype(jnp.bfloat16)
        low = (part - high.astype(jnp.float32)).astype(jnp.bfloat16)
        left = jnp.concatenate([high, high, low], axis=1)
        out_ref[:height] += jnp.dot(left, right, preferred_element_type=jnp.float32)
    half = mine_ref.shape[0]
    mine_ref[...] = out_ref[pl.ds(pl.multiple_of(core_ref[0] * half, half), half)]
    other_ref[...] = out_ref[pl.ds(pl.multiple_of((1 - core_ref[0]) * half, half), half)]


def gradient(features, core, rows, out_rows):
    width = rows.shape[2]
    return pl.pallas_call(
        gradient_kernel,
        in_specs=[VMEM] * len(features) + [SMEM, VMEM],
        out_specs=[VMEM] * 2,
        out_shape=[pltpu.VMEM((out_rows // 2, width), jnp.float32)] * 2,
        scratch_shapes=[pltpu.VMEM((out_rows, width), jnp.float32)],
        compiler_params=pltpu.CompilerParams(vmem_limit_bytes=VMEM_LIMIT),
        cost_estimate=pl.CostEstimate(
            flops=6 * out_rows * rows.shape[0] * TILE * width, bytes_accessed=10**7, transcendentals=0
        ),
    )(*[in_vmem(f) for f in features], core.reshape(1), in_vmem(rows))


def exchange(value, axes):
    return lax.all_to_all(value, axes, 0, 0, tiled=True)


def gather(value, axes):
    return exchange(jnp.broadcast_to(value, (lax.axis_size(axes),) + value.shape), axes)


def swap(value, axis):
    return lax.ppermute(value, axis, [(0, 1), (1, 0)])


def from_ahead(value, axis, steps):
    size = lax.axis_size(axis)
    return lax.ppermute(value, axis, [(i, (i - steps) % size) for i in range(size)])


def sum_everywhere(mine, other):
    rows, width = mine.shape
    mine = mine + swap(other, "core")
    own = exchange(mine.reshape(-1, rows // lax.axis_size(("x", "zl")), width), ("x", "zl")).sum(0)
    own = gather(own, REP).sum(0)
    mine = gather(own, ("x", "zl")).reshape(rows, width)
    other = swap(mine, "core")
    return jnp.where(
        lax.axis_index("core") == 0, jnp.concatenate([mine, other]), jnp.concatenate([other, mine])
    )


def local(features, weight, cotangent, degree, tile_row, tile_col, edge_dst, edge_src, tile_live):
    own_rows, in_width = features.shape
    hidden_width = weight.shape[1]
    own_blocks = own_rows // TILE
    group_blocks = own_blocks * lax.axis_size(REP)
    half_blocks = own_blocks * lax.axis_size(("x", "zl"))
    blocks = (-1, TILE, hidden_width)
    scales = lax.rsqrt(degree.astype(jnp.float32))[:, None]
    row_ids = tile_row.reshape(-1)
    live = tile_live.reshape(1)
    slots, edges = edge_dst.shape[2:]
    owner, within = tile_col.reshape(-1) // own_blocks, tile_col.reshape(-1) % own_blocks
    other_core = owner % 2 ^ lax.axis_index("core")
    from_ids = other_core * half_blocks + owner // 2 * own_blocks + within
    x_ahead = (owner // 4 - lax.axis_index("x")) % 4
    other_z = owner // 2 % 2 ^ lax.axis_index("zl")
    to_ids = other_core * half_blocks + (x_ahead * 2 + other_z) * own_blocks + within

    scaled = jnp.dot(features, weight, precision=HIGH, preferred_element_type=jnp.float32) * scales
    height = -(-in_width // 32) * 32
    here = jnp.pad(features.T * scales.T, ((0, height - in_width), (0, 0)))
    wide_scales = jnp.broadcast_to(scales, (own_rows, TILE))
    scaled, here, wide_scales = lax.optimization_barrier((scaled, here, wide_scales))
    near = gather(scaled, ("x", "zl"))
    here, near = lax.optimization_barrier((here, near))
    far = swap(near, "core")
    across = swap(here, "zl")
    here_x = [from_ahead(here, "x", steps) for steps in (1, 2, 3)]
    tiles = build_tiles(live, edge_dst.reshape(slots, edges), edge_src.reshape(slots, edges))

    def forward(near, far, scaled, cotangent, wide_scales):
        sources = [near.reshape(blocks), far.reshape(blocks)]
        (sums,) = aggregate(tiles, live, from_ids, row_ids, sources, [group_blocks], False)
        return activate(exchange(sums.reshape(-1, own_rows, hidden_width), REP), scaled, cotangent, wide_scales)

    def never(near, far, scaled, cotangent, wide_scales):
        return scaled + cotangent, scaled - cotangent

    hidden, back_own = lax.cond(live[0] > 0, forward, never, near, far, scaled, cotangent, wide_scales)
    across, here_x, back_own = lax.optimization_barrier((across, here_x, back_own))
    across_x = [from_ahead(across, "x", steps) for steps in (1, 2, 3)]
    back_group = lax.cond(
        live[0] > 0,
        lambda back: gather(back, REP),
        lambda back: jnp.broadcast_to(back, (lax.axis_size(REP),) + back.shape),
        back_own,
    )
    across_x, back_group = lax.optimization_barrier((across_x, back_group))
    kept, sent = aggregate(
        tiles, live, row_ids, to_ids, [back_group.reshape(blocks)], [half_blocks] * 2, True
    )
    kept = kept + swap(sent, "core")
    kept = kept + jnp.pad(back_own.reshape(blocks), ((0, half_blocks - own_blocks), (0, 0), (0, 0)))
    held = [part for pair in zip([here, *here_x], [across, *across_x]) for part in pair]
    parts = lax.axis_size(BLK)
    out_rows = -(-in_width // (8 * parts)) * 8 * parts
    halves = gradient(held, lax.axis_index("core"), kept, out_rows)
    return (hidden, sum_everywhere(*halves)[:in_width])


def solution(mesh):
    mesh = Mesh(mesh.devices.reshape(4, 2, 2, 4, 2), BLK + REP)
    nodes = P(BLK + REP)
    tile = P(BLK, REP)
    return jax.shard_map(
        local,
        mesh=mesh,
        in_specs=(nodes, P(), nodes, nodes, tile, tile, tile, tile, tile),
        out_specs=(nodes, P()),
        check_vma=False,
    )
```

```python
from functools import partial

import jax
import jax.numpy as jnp
from jax import lax
from jax.experimental import pallas as pl
from jax.experimental.pallas import tpu as pltpu
from jax.sharding import Mesh
from jax.sharding import PartitionSpec as P

TILE = 128
HIGH = lax.Precision.HIGHEST
activation = partial(jax.nn.gelu, approximate=True)
ROWS = 32
PIECE = 3
PARTS = 2
AHEAD = 2
STRIP = 128
UNROLL = 32
VMEM_LIMIT = 32 * 1024 * 1024
BLK = ("x", "zl", "core")
REP = ("y", "zh")


def in_vmem(value):
    return pltpu.with_memory_space_constraint(value, pltpu.VMEM)


def in_hbm(value):
    return pltpu.with_memory_space_constraint(value, pltpu.HBM)


SMEM = pl.BlockSpec(memory_space=pltpu.SMEM)
VMEM = pl.BlockSpec(memory_space=pltpu.VMEM)
ANY = pl.BlockSpec(memory_space=pl.ANY)


def tile_kernel(live_ref, dst_hbm, src_hbm, out_ref, dst_ref, src_ref, tiles, edge_sems, sems):
    live = live_ref[0]
    groups = (live + ROWS - 1) // ROWS
    node_ids = lax.broadcasted_iota(jnp.int32, (TILE, dst_ref.shape[1]), 0).astype(jnp.float32).astype(jnp.bfloat16)
    one, zero = jnp.ones((), jnp.bfloat16), jnp.zeros((), jnp.bfloat16)

    def one_hot(ids):
        hot = ids.astype(jnp.float32).astype(jnp.bfloat16) == node_ids
        return jnp.where(hot, one, zero).astype(jnp.float8_e4m3fn)

    def copies_in(group):
        at = pl.ds(pl.multiple_of(group * ROWS, ROWS), ROWS)
        return [
            pltpu.make_async_copy(dst_hbm.at[at], dst_ref.at[at], edge_sems.at[0, group]),
            pltpu.make_async_copy(src_hbm.at[at], src_ref.at[at], edge_sems.at[1, group]),
        ]

    def start_in(group, carry):
        for copy in copies_in(group):
            copy.start()
        return carry

    def copy_out(group):
        at = pl.ds(pl.multiple_of(group * ROWS, ROWS), ROWS)
        return pltpu.make_async_copy(tiles.at[at], out_ref.at[at], sems.at[group])

    def some_slots(group, carry):
        for copy in copies_in(group):
            copy.wait()
        first = pl.multiple_of(group * ROWS, ROWS)
        dst = dst_ref[pl.ds(first, ROWS)]
        src = src_ref[pl.ds(first, ROWS)]
        for k in range(ROWS):
            dst_ids = jnp.where(first + k < live, dst[k : k + 1], TILE)
            counts = lax.dot_general(
                one_hot(dst_ids),
                one_hot(src[k : k + 1]),
                (((1,), (1,)), ((), ())),
                preferred_element_type=jnp.float32,
            )
            tiles[first + k] = counts.astype(jnp.bfloat16)
        copy_out(group).start()
        return carry

    lax.fori_loop(0, groups, start_in, 0)
    lax.fori_loop(0, groups, some_slots, 0)
    lax.fori_loop(0, groups, lambda group, carry: (copy_out(group).wait(), carry)[1], 0)


def build_tiles(live, edge_dst, edge_src):
    slots, edges = edge_dst.shape
    return pl.pallas_call(
        tile_kernel,
        in_specs=[SMEM, ANY, ANY],
        out_specs=ANY,
        out_shape=pltpu.HBM((slots, TILE, TILE), jnp.bfloat16),
        scratch_shapes=[
            pltpu.VMEM((slots, edges), jnp.int32),
            pltpu.VMEM((slots, edges), jnp.int32),
            pltpu.VMEM((slots, TILE, TILE), jnp.bfloat16),
            pltpu.SemaphoreType.DMA((2, slots // ROWS)),
            pltpu.SemaphoreType.DMA((slots // ROWS,)),
        ],
        compiler_params=pltpu.CompilerParams(vmem_limit_bytes=VMEM_LIMIT),
        cost_estimate=pl.CostEstimate(flops=10**6, bytes_accessed=10**5, transcendentals=0),
    )(live, in_hbm(edge_dst), in_hbm(edge_src))


def aggregate_kernel(parts, targets, transpose, live_ref, pick_ref, place_ref, own_ref, tiles_ref, *refs):
    sources, outs = refs[:parts], refs[parts : parts + targets]
    split, landed, tiles, sems, tile_sems, *more = refs[parts + targets :]
    totals = more[0] if more else outs[0]
    groups = (live_ref[0] + UNROLL - 1) // UNROLL

    def tile_copy(group):
        at = pl.ds(pl.multiple_of(group * UNROLL, UNROLL), UNROLL)
        return pltpu.make_async_copy(tiles_ref.at[at], tiles.at[at], tile_sems.at[group])

    pieces = [
        (p, b) for p, source_ref in enumerate(sources) for b in range(0, source_ref.shape[0], PIECE)
    ]
    copies = []
    for n, (p, b) in enumerate(pieces):
        copy = pltpu.make_async_copy(
            sources[p].at[pl.ds(b, PIECE)], landed.at[pl.ds(n * PIECE, PIECE)], sems.at[n]
        )
        copy.start()
        copies.append(copy)
    for group in range(AHEAD):
        pl.when(group < groups)(tile_copy(group).start)
    totals[...] = jnp.zeros_like(totals)

    for n, copy in enumerate(copies):
        copy.wait()
        if not transpose:

            @pl.when(own_ref[1] == n * PIECE)
            def _():
                totals[pl.ds(own_ref[0], PIECE)] = landed[n * PIECE : (n + 1) * PIECE]

        def split_block(k, carry):
            value = landed[n * PIECE + k]
            high = value.astype(jnp.bfloat16)
            split[n * PIECE + k, :TILE] = high
            split[n * PIECE + k, TILE:] = (value - high.astype(jnp.float32)).astype(jnp.bfloat16)
            return carry

        lax.fori_loop(0, PIECE, split_block, 0)

    def some_tiles(group, carry):
        tile_copy(group).wait()
        pl.when(group + AHEAD < groups)(lambda: tile_copy(group + AHEAD).start())
        first = group * UNROLL
        products = []
        for k in range(UNROLL):
            tile = tiles[first + k]
            picked = split[pick_ref[first + k]]
            twice = jnp.concatenate([tile, tile], axis=0 if transpose else 1)
            products.append(
                lax.dot_general(
                    twice,
                    picked,
                    (((0 if transpose else 1,), (0,)), ((), ())),
                    preferred_element_type=jnp.float32,
                )
            )
        for k in range(UNROLL):
            totals[place_ref[first + k]] += products[k]
        return carry

    lax.fori_loop(0, groups, some_tiles, 0)
    if more:
        for p, out_ref in enumerate(outs):
            count = out_ref.shape[0]
            out_ref[...] = totals[p * count : (p + 1) * count]


def aggregate(tiles, live, pick_ids, place_ids, own, sources, target_blocks, transpose):
    slots = tiles.shape[0]
    source_blocks, _, width = sources[0].shape
    parts, targets = len(sources), len(target_blocks)
    return pl.pallas_call(
        partial(aggregate_kernel, parts, targets, transpose),
        in_specs=[SMEM] * 4 + [ANY] * (1 + parts),
        out_specs=[VMEM] * targets,
        out_shape=[pltpu.VMEM((b, TILE, width), jnp.float32) for b in target_blocks],
        scratch_shapes=[
            pltpu.VMEM((parts * source_blocks, 2 * TILE, width), jnp.bfloat16),
            pltpu.VMEM((parts * source_blocks, TILE, width), jnp.float32),
            pltpu.VMEM(tiles.shape, jnp.bfloat16),
            pltpu.SemaphoreType.DMA((parts * source_blocks // PIECE,)),
            pltpu.SemaphoreType.DMA((slots // UNROLL,)),
        ]
        + [pltpu.VMEM((sum(target_blocks), TILE, width), jnp.float32)] * (targets > 1),
        compiler_params=pltpu.CompilerParams(vmem_limit_bytes=VMEM_LIMIT),
        cost_estimate=pl.CostEstimate(
            flops=10**6, bytes_accessed=10**5, transcendentals=0
        ),
    )(live, pick_ids, place_ids, own, in_hbm(tiles), *sources)


def activate_kernel(parts_ref, cotangent_ref, scales_ref, hidden_ref, back_ref):
    scales = jnp.concatenate([scales_ref[...]] * (hidden_ref.shape[1] // TILE), axis=1)
    pre = parts_ref[...].sum(0) * scales
    hidden, pull = jax.vjp(activation, pre)
    hidden_ref[...] = hidden
    back_ref[...] = pull(cotangent_ref[...])[0] * scales


def activate(parts, cotangent, scales):
    count, rows, width = parts.shape
    block = pl.BlockSpec((STRIP, width), lambda g: (g, 0))
    return pl.pallas_call(
        activate_kernel,
        grid=(rows // STRIP,),
        in_specs=[
            pl.BlockSpec((count, STRIP, width), lambda g: (0, g, 0)),
            block,
            pl.BlockSpec((STRIP, TILE), lambda g: (g, 0)),
        ],
        out_specs=[block, block],
        out_shape=[jax.ShapeDtypeStruct((rows, width), jnp.float32)] * 2,
        compiler_params=pltpu.CompilerParams(vmem_limit_bytes=VMEM_LIMIT),
    )(parts, cotangent, scales)


def project_kernel(features_ref, weight_ref, degree_ref, scaled_ref, turned_ref, scales_ref, padded):
    height, in_width = turned_ref.shape[0], features_ref.shape[0]
    scales = lax.rsqrt(degree_ref[...].astype(jnp.float32))
    turned_ref[:in_width] = features_ref[...] * scales
    turned_ref[in_width:] = jnp.zeros((height - in_width, turned_ref.shape[1]), jnp.float32)
    padded[:in_width] = weight_ref[...]
    padded[in_width:] = jnp.zeros((height - in_width, padded.shape[1]), jnp.float32)
    left_high, left_low = two_terms(turned_ref[...])
    right_high, right_low = two_terms(padded[...])
    scaled_ref[...] = lax.dot_general(
        jnp.concatenate([left_high, left_high, left_low]),
        jnp.concatenate([right_high, right_low, right_high]),
        (((0,), (0,)), ((), ())),
        preferred_element_type=jnp.float32,
    )
    scales_ref[...] = jnp.broadcast_to(scales, (TILE, scales.shape[1])).T


def two_terms(value):
    high = value.astype(jnp.bfloat16)
    return high, (value - high.astype(jnp.float32)).astype(jnp.bfloat16)


def project(features, weight, degree, height):
    in_width, rows = features.shape
    width = weight.shape[1]
    return pl.pallas_call(
        project_kernel,
        in_specs=[VMEM] * 3,
        out_specs=[VMEM] * 3,
        out_shape=[
            jax.ShapeDtypeStruct((rows, width), jnp.float32),
            jax.ShapeDtypeStruct((height, rows), jnp.float32),
            jax.ShapeDtypeStruct((rows, TILE), jnp.float32),
        ],
        scratch_shapes=[pltpu.VMEM((height, width), jnp.float32)],
        compiler_params=pltpu.CompilerParams(vmem_limit_bytes=VMEM_LIMIT),
    )(features, weight, degree.reshape(1, rows))


def split_features_kernel(*refs):
    features, (high_ref, low_ref) = refs[:-2], refs[-2:]
    nodes = features[0].shape[1]
    for p, part_ref in enumerate(features):
        at = pl.ds(p % PARTS * nodes, nodes)
        high, low = two_terms(part_ref[...])
        high_ref[p // PARTS, :, at] = high
        low_ref[p // PARTS, :, at] = low


def split_features(features):
    height, nodes = features[0].shape
    shape = (len(features) // PARTS, height, PARTS * nodes)
    return pl.pallas_call(
        split_features_kernel,
        in_specs=[VMEM] * len(features),
        out_specs=[VMEM] * 2,
        out_shape=[pltpu.VMEM(shape, jnp.bfloat16)] * 2,
        compiler_params=pltpu.CompilerParams(vmem_limit_bytes=VMEM_LIMIT),
        cost_estimate=pl.CostEstimate(flops=10**6, bytes_accessed=10**7, transcendentals=0),
    )(*[in_vmem(f) for f in features])


def gradient_kernel(core_ref, high_ref, low_ref, rows_ref, mine_ref, other_ref, out_ref):
    parts, height, nodes = high_ref.shape
    blocks = nodes // TILE
    out_ref[...] = jnp.zeros_like(out_ref)
    for p in range(parts):
        rows = rows_ref[p * blocks : (p + 1) * blocks].reshape(nodes, out_ref.shape[1])
        rows_high, rows_low = two_terms(rows)
        right = jnp.concatenate([rows_high, rows_low, rows_high], axis=0)
        left = jnp.concatenate([high_ref[p], high_ref[p], low_ref[p]], axis=1)
        out_ref[:height] += jnp.dot(left, right, preferred_element_type=jnp.float32)
    half = mine_ref.shape[0]
    mine_ref[...] = out_ref[pl.ds(pl.multiple_of(core_ref[0] * half, half), half)]
    other_ref[...] = out_ref[pl.ds(pl.multiple_of((1 - core_ref[0]) * half, half), half)]


def gradient(features, core, rows, out_rows):
    high, low = features
    width = rows.shape[2]
    return pl.pallas_call(
        gradient_kernel,
        in_specs=[SMEM] + [VMEM] * 3,
        out_specs=[VMEM] * 2,
        out_shape=[pltpu.VMEM((out_rows // 2, width), jnp.float32)] * 2,
        scratch_shapes=[pltpu.VMEM((out_rows, width), jnp.float32)],
        compiler_params=pltpu.CompilerParams(vmem_limit_bytes=VMEM_LIMIT),
        cost_estimate=pl.CostEstimate(
            flops=6 * out_rows * rows.shape[0] * TILE * width, bytes_accessed=10**7, transcendentals=0
        ),
    )(core.reshape(1), in_vmem(high), in_vmem(low), in_vmem(rows))


def exchange(value, axes):
    return lax.all_to_all(value, axes, 0, 0, tiled=True)


def gather(value, axes):
    return exchange(jnp.broadcast_to(value, (lax.axis_size(axes),) + value.shape), axes)


def swap(value, axis):
    return lax.ppermute(value, axis, [(0, 1), (1, 0)])


def from_ahead(value, axis, steps):
    size = lax.axis_size(axis)
    return lax.ppermute(value, axis, [(i, (i - steps) % size) for i in range(size)])


def sum_everywhere(mine, other):
    rows, width = mine.shape
    mine = mine + swap(other, "core")
    own = exchange(mine.reshape(-1, rows // lax.axis_size(("x", "zl")), width), ("x", "zl")).sum(0)
    own = gather(own, REP).sum(0)
    mine = gather(own, ("x", "zl")).reshape(rows, width)
    other = swap(mine, "core")
    return jnp.where(
        lax.axis_index("core") == 0, jnp.concatenate([mine, other]), jnp.concatenate([other, mine])
    )


def local(features, weight, cotangent, degree, tile_row, tile_col, edge_dst, edge_src, tile_live):
    own_rows, in_width = features.shape
    hidden_width = weight.shape[1]
    own_blocks = own_rows // TILE
    group_blocks = own_blocks * lax.axis_size(REP)
    half_blocks = own_blocks * lax.axis_size(("x", "zl"))
    blocks = (-1, TILE, hidden_width)
    row_ids = tile_row.reshape(-1)
    live = tile_live.reshape(1)
    slots, edges = edge_dst.shape[2:]
    owner, within = tile_col.reshape(-1) // own_blocks, tile_col.reshape(-1) % own_blocks
    other_core = owner % 2 ^ lax.axis_index("core")
    from_ids = other_core * half_blocks + owner // 2 * own_blocks + within
    x_ahead = (owner // 4 - lax.axis_index("x")) % 4
    other_z = owner // 2 % 2 ^ lax.axis_index("zl")
    to_ids = other_core * half_blocks + (x_ahead * 2 + other_z) * own_blocks + within

    height = -(-in_width // 32) * 32
    scaled, here, scales = project(features.T, weight, degree, height)
    scaled, here, scales = lax.optimization_barrier((scaled, here, scales))
    near = gather(scaled, ("x", "zl"))
    here, near = lax.optimization_barrier((here, near))
    far = swap(near, "core")
    across = swap(here, "zl")
    here_x = [from_ahead(here, "x", steps) for steps in (1, 2, 3)]
    tiles = build_tiles(live, edge_dst.reshape(slots, edges), edge_src.reshape(slots, edges))

    own_source = (lax.axis_index(("x", "zl")) * own_blocks).reshape(1)
    own = jnp.concatenate([(lax.axis_index(REP) * own_blocks).reshape(1), own_source]).astype(jnp.int32)

    def forward(near, far, cotangent, scales):
        sources = [near.reshape(blocks), far.reshape(blocks)]
        (sums,) = aggregate(tiles, live, from_ids, row_ids, own, sources, [group_blocks], False)
        return activate(exchange(sums.reshape(-1, own_rows, hidden_width), REP), cotangent, scales)

    def never(near, far, cotangent, scales):
        return near[0] + cotangent, far[0] - cotangent

    hidden, back_own = lax.cond(live[0] > 0, forward, never, near, far, cotangent, scales)
    across, here_x, back_own = lax.optimization_barrier((across, here_x, back_own))
    across_x = [from_ahead(across, "x", steps) for steps in (1, 2, 3)]
    back_group = lax.cond(
        live[0] > 0,
        lambda back: gather(back, REP),
        lambda back: jnp.broadcast_to(back, (lax.axis_size(REP),) + back.shape),
        back_own,
    )
    across_x, back_group = lax.optimization_barrier((across_x, back_group))
    kept, sent = aggregate(
        tiles, live, row_ids, to_ids, own, [back_group.reshape(blocks)], [half_blocks] * 2, True
    )
    kept = kept + swap(sent, "core")
    kept = kept + jnp.pad(back_own.reshape(blocks), ((0, half_blocks - own_blocks), (0, 0), (0, 0)))
    held = [part for pair in zip([here, *here_x], [across, *across_x]) for part in pair]
    parts = lax.axis_size(BLK)
    out_rows = -(-in_width // (8 * parts)) * 8 * parts
    halves = gradient(split_features(held), lax.axis_index("core"), kept, out_rows)
    return (hidden, sum_everywhere(*halves)[:in_width])


def solution(mesh):
    mesh = Mesh(mesh.devices.reshape(4, 2, 2, 4, 2), BLK + REP)
    nodes = P(BLK + REP)
    tile = P(BLK, REP)
    return jax.shard_map(
        local,
        mesh=mesh,
        in_specs=(nodes, P(), nodes, nodes, tile, tile, tile, tile, tile),
        out_specs=(nodes, P()),
        check_vma=False,
    )
```

```python
from functools import partial

import jax
import jax.numpy as jnp
from jax import lax
from jax.experimental import pallas as pl
from jax.experimental.pallas import tpu as pltpu
from jax.sharding import Mesh
from jax.sharding import PartitionSpec as P

TILE = 128
HIGH = lax.Precision.HIGHEST
activation = partial(jax.nn.gelu, approximate=True)
ROWS = 32
PIECE = 3
PARTS = 2
AHEAD = 2
STRIP = 128
UNROLL = 32
VMEM_LIMIT = 28 * 1024 * 1024
BLK = ("x", "zl", "core")
REP = ("y", "zh")


def in_vmem(value):
    return pltpu.with_memory_space_constraint(value, pltpu.VMEM)


def in_hbm(value):
    return pltpu.with_memory_space_constraint(value, pltpu.HBM)


SMEM = pl.BlockSpec(memory_space=pltpu.SMEM)
VMEM = pl.BlockSpec(memory_space=pltpu.VMEM)
ANY = pl.BlockSpec(memory_space=pl.ANY)


def tile_kernel(live_ref, dst_hbm, src_hbm, out_ref, dst_ref, src_ref, tiles, edge_sems, sems):
    live = live_ref[0]
    groups = (live + ROWS - 1) // ROWS
    node_ids = lax.broadcasted_iota(jnp.int32, (TILE, dst_ref.shape[1]), 0).astype(jnp.float32).astype(jnp.bfloat16)
    one, zero = jnp.ones((), jnp.bfloat16), jnp.zeros((), jnp.bfloat16)

    def one_hot(ids):
        hot = ids.astype(jnp.float32).astype(jnp.bfloat16) == node_ids
        return jnp.where(hot, one, zero).astype(jnp.float8_e4m3fn)

    def copies_in(group):
        at = pl.ds(pl.multiple_of(group * ROWS, ROWS), ROWS)
        return [
            pltpu.make_async_copy(dst_hbm.at[at], dst_ref.at[at], edge_sems.at[0, group]),
            pltpu.make_async_copy(src_hbm.at[at], src_ref.at[at], edge_sems.at[1, group]),
        ]

    def start_in(group, carry):
        for copy in copies_in(group):
            copy.start()
        return carry

    def copy_out(group):
        at = pl.ds(pl.multiple_of(group * ROWS, ROWS), ROWS)
        return pltpu.make_async_copy(tiles.at[at], out_ref.at[at], sems.at[group])

    def some_slots(group, carry):
        for copy in copies_in(group):
            copy.wait()
        first = pl.multiple_of(group * ROWS, ROWS)
        dst = dst_ref[pl.ds(first, ROWS)]
        src = src_ref[pl.ds(first, ROWS)]
        for k in range(ROWS):
            dst_ids = jnp.where(first + k < live, dst[k : k + 1], TILE)
            counts = lax.dot_general(
                one_hot(dst_ids),
                one_hot(src[k : k + 1]),
                (((1,), (1,)), ((), ())),
                preferred_element_type=jnp.float32,
            )
            tiles[first + k] = counts.astype(jnp.bfloat16)
        copy_out(group).start()
        return carry

    lax.fori_loop(0, groups, start_in, 0)
    lax.fori_loop(0, groups, some_slots, 0)
    lax.fori_loop(0, groups, lambda group, carry: (copy_out(group).wait(), carry)[1], 0)


def build_tiles(live, edge_dst, edge_src):
    slots, edges = edge_dst.shape
    return pl.pallas_call(
        tile_kernel,
        in_specs=[SMEM, ANY, ANY],
        out_specs=ANY,
        out_shape=pltpu.HBM((slots, TILE, TILE), jnp.bfloat16),
        scratch_shapes=[
            pltpu.VMEM((slots, edges), jnp.int32),
            pltpu.VMEM((slots, edges), jnp.int32),
            pltpu.VMEM((slots, TILE, TILE), jnp.bfloat16),
            pltpu.SemaphoreType.DMA((2, slots // ROWS)),
            pltpu.SemaphoreType.DMA((slots // ROWS,)),
        ],
        compiler_params=pltpu.CompilerParams(vmem_limit_bytes=VMEM_LIMIT),
        cost_estimate=pl.CostEstimate(flops=10**6, bytes_accessed=10**5, transcendentals=0),
    )(live, in_hbm(edge_dst), in_hbm(edge_src))


def aggregate_kernel(parts, targets, transpose, live_ref, pick_ref, place_ref, own_ref, tiles_ref, *refs):
    sources, outs = refs[:parts], refs[parts : parts + targets]
    split, landed, tiles, sems, tile_sems, *more = refs[parts + targets :]
    totals = more[0] if more else outs[0]
    groups = (live_ref[0] + UNROLL - 1) // UNROLL

    def tile_copy(group):
        at = pl.ds(pl.multiple_of(group * UNROLL, UNROLL), UNROLL)
        return pltpu.make_async_copy(tiles_ref.at[at], tiles.at[at], tile_sems.at[group])

    pieces = [
        (p, b) for p, source_ref in enumerate(sources) for b in range(0, source_ref.shape[0], PIECE)
    ]
    copies = []
    for n, (p, b) in enumerate(pieces):
        copy = pltpu.make_async_copy(
            sources[p].at[pl.ds(b, PIECE)], landed.at[pl.ds(n * PIECE, PIECE)], sems.at[n]
        )
        copy.start()
        copies.append(copy)
    for group in range(AHEAD):
        pl.when(group < groups)(tile_copy(group).start)
    totals[...] = jnp.zeros_like(totals)

    for n, copy in enumerate(copies):
        copy.wait()
        if not transpose:

            @pl.when(own_ref[1] == n * PIECE)
            def _():
                totals[pl.ds(own_ref[0], PIECE)] = landed[n * PIECE : (n + 1) * PIECE]

        def split_block(k, carry):
            value = landed[n * PIECE + k]
            high = value.astype(jnp.bfloat16)
            split[n * PIECE + k, :TILE] = high
            split[n * PIECE + k, TILE:] = (value - high.astype(jnp.float32)).astype(jnp.bfloat16)
            return carry

        lax.fori_loop(0, PIECE, split_block, 0)

    def some_tiles(group, carry):
        tile_copy(group).wait()
        pl.when(group + AHEAD < groups)(lambda: tile_copy(group + AHEAD).start())
        first = group * UNROLL
        products = []
        for k in range(UNROLL):
            tile = tiles[first + k]
            picked = split[pick_ref[first + k]]
            twice = jnp.concatenate([tile, tile], axis=0 if transpose else 1)
            products.append(
                lax.dot_general(
                    twice,
                    picked,
                    (((0 if transpose else 1,), (0,)), ((), ())),
                    preferred_element_type=jnp.float32,
                )
            )
        for k in range(UNROLL):
            totals[place_ref[first + k]] += products[k]
        return carry

    lax.fori_loop(0, groups, some_tiles, 0)
    if more:
        for p, out_ref in enumerate(outs):
            count = out_ref.shape[0]
            out_ref[...] = totals[p * count : (p + 1) * count]


def aggregate(tiles, live, pick_ids, place_ids, own, sources, target_blocks, transpose):
    slots = tiles.shape[0]
    source_blocks, _, width = sources[0].shape
    parts, targets = len(sources), len(target_blocks)
    return pl.pallas_call(
        partial(aggregate_kernel, parts, targets, transpose),
        in_specs=[SMEM] * 4 + [ANY] * (1 + parts),
        out_specs=[VMEM] * targets,
        out_shape=[pltpu.VMEM((b, TILE, width), jnp.float32) for b in target_blocks],
        scratch_shapes=[
            pltpu.VMEM((parts * source_blocks, 2 * TILE, width), jnp.bfloat16),
            pltpu.VMEM((parts * source_blocks, TILE, width), jnp.float32),
            pltpu.VMEM(tiles.shape, jnp.bfloat16),
            pltpu.SemaphoreType.DMA((parts * source_blocks // PIECE,)),
            pltpu.SemaphoreType.DMA((slots // UNROLL,)),
        ]
        + [pltpu.VMEM((sum(target_blocks), TILE, width), jnp.float32)] * (targets > 1),
        compiler_params=pltpu.CompilerParams(vmem_limit_bytes=VMEM_LIMIT),
        cost_estimate=pl.CostEstimate(
            flops=10**6, bytes_accessed=10**5, transcendentals=0
        ),
    )(live, pick_ids, place_ids, own, in_hbm(tiles), *sources)


def activate_kernel(parts_ref, cotangent_ref, scales_ref, hidden_ref, back_ref):
    scales = jnp.concatenate([scales_ref[...]] * (hidden_ref.shape[1] // TILE), axis=1)
    pre = parts_ref[...].sum(0) * scales
    hidden, pull = jax.vjp(activation, pre)
    hidden_ref[...] = hidden
    back_ref[...] = pull(cotangent_ref[...])[0] * scales


def activate(parts, cotangent, scales):
    count, rows, width = parts.shape
    block = pl.BlockSpec((STRIP, width), lambda g: (g, 0))
    return pl.pallas_call(
        activate_kernel,
        grid=(rows // STRIP,),
        in_specs=[
            pl.BlockSpec((count, STRIP, width), lambda g: (0, g, 0)),
            block,
            pl.BlockSpec((STRIP, TILE), lambda g: (g, 0)),
        ],
        out_specs=[block, block],
        out_shape=[jax.ShapeDtypeStruct((rows, width), jnp.float32)] * 2,
        compiler_params=pltpu.CompilerParams(vmem_limit_bytes=VMEM_LIMIT),
    )(parts, cotangent, scales)


def project_kernel(
    features_hbm,
    weight_hbm,
    degree_hbm,
    scaled_ref,
    turned_ref,
    scales_ref,
    features_ref,
    weight_ref,
    degree_ref,
    padded,
    sems,
):
    height, in_width = turned_ref.shape[0], features_ref.shape[0]
    features_in = pltpu.make_async_copy(features_hbm, features_ref, sems.at[0])
    weight_in = pltpu.make_async_copy(weight_hbm, weight_ref, sems.at[1])
    degree_in = pltpu.make_async_copy(degree_hbm, degree_ref, sems.at[2])
    degree_in.start()
    features_in.start()
    weight_in.start()
    degree_in.wait()
    scales = lax.rsqrt(degree_ref[...].astype(jnp.float32)).reshape(1, -1)
    features_in.wait()
    turned_ref[:in_width] = features_ref[...] * scales
    turned_ref[in_width:] = jnp.zeros((height - in_width, turned_ref.shape[1]), jnp.float32)
    weight_in.wait()
    padded[:in_width] = weight_ref[...]
    padded[in_width:] = jnp.zeros((height - in_width, padded.shape[1]), jnp.float32)
    left_high, left_low = two_terms(turned_ref[...])
    right_high, right_low = two_terms(padded[...])
    scaled_ref[...] = lax.dot_general(
        jnp.concatenate([left_high, left_high, left_low]),
        jnp.concatenate([right_high, right_low, right_high]),
        (((0,), (0,)), ((), ())),
        preferred_element_type=jnp.float32,
    )
    scales_ref[...] = jnp.broadcast_to(scales, (TILE, scales.shape[1])).T


def two_terms(value):
    high = value.astype(jnp.bfloat16)
    return high, (value - high.astype(jnp.float32)).astype(jnp.bfloat16)


def project(features, weight, degree, height):
    in_width, rows = features.shape
    width = weight.shape[1]
    return pl.pallas_call(
        project_kernel,
        in_specs=[ANY] * 3,
        out_specs=[VMEM] * 3,
        out_shape=[
            jax.ShapeDtypeStruct((rows, width), jnp.float32),
            jax.ShapeDtypeStruct((height, rows), jnp.float32),
            jax.ShapeDtypeStruct((rows, TILE), jnp.float32),
        ],
        scratch_shapes=[
            pltpu.VMEM(features.shape, jnp.float32),
            pltpu.VMEM(weight.shape, jnp.float32),
            pltpu.VMEM(degree.shape, jnp.int32),
            pltpu.VMEM((height, width), jnp.float32),
            pltpu.SemaphoreType.DMA((3,)),
        ],
        compiler_params=pltpu.CompilerParams(vmem_limit_bytes=VMEM_LIMIT),
    )(in_hbm(features), in_hbm(weight), in_hbm(degree))


def split_features_kernel(*refs):
    features, (high_ref, low_ref) = refs[:-2], refs[-2:]
    nodes = features[0].shape[1]
    for p, part_ref in enumerate(features):
        at = pl.ds(p % PARTS * nodes, nodes)
        high, low = two_terms(part_ref[...])
        high_ref[p // PARTS, :, at] = high
        low_ref[p // PARTS, :, at] = low


def split_features(features):
    height, nodes = features[0].shape
    shape = (len(features) // PARTS, height, PARTS * nodes)
    return pl.pallas_call(
        split_features_kernel,
        in_specs=[VMEM] * len(features),
        out_specs=[VMEM] * 2,
        out_shape=[pltpu.VMEM(shape, jnp.bfloat16)] * 2,
        compiler_params=pltpu.CompilerParams(vmem_limit_bytes=VMEM_LIMIT),
        cost_estimate=pl.CostEstimate(flops=10**6, bytes_accessed=10**7, transcendentals=0),
    )(*[in_vmem(f) for f in features])


def gradient_kernel(core_ref, high_ref, low_ref, kept_ref, came_ref, own_ref, mine_ref, other_ref, out_ref):
    parts, height, nodes = high_ref.shape
    blocks = nodes // TILE
    out_ref[...] = jnp.zeros_like(out_ref)
    for p in range(parts):
        rows = kept_ref[p * blocks : (p + 1) * blocks] + came_ref[p * blocks : (p + 1) * blocks]
        if p == 0:
            own = own_ref.shape[0]
            rows = jnp.concatenate([rows[:own] + own_ref[...], rows[own:]])
        rows = rows.reshape(nodes, out_ref.shape[1])
        rows_high, rows_low = two_terms(rows)
        right = jnp.concatenate([rows_high, rows_low, rows_high], axis=0)
        left = jnp.concatenate([high_ref[p], high_ref[p], low_ref[p]], axis=1)
        out_ref[:height] += jnp.dot(left, right, preferred_element_type=jnp.float32)
    half = mine_ref.shape[0]
    mine_ref[...] = out_ref[pl.ds(pl.multiple_of(core_ref[0] * half, half), half)]
    other_ref[...] = out_ref[pl.ds(pl.multiple_of((1 - core_ref[0]) * half, half), half)]


def gradient(features, core, kept, came, own, out_rows):
    high, low = features
    width = kept.shape[2]
    return pl.pallas_call(
        gradient_kernel,
        in_specs=[SMEM] + [VMEM] * 5,
        out_specs=[VMEM] * 2,
        out_shape=[pltpu.VMEM((out_rows // 2, width), jnp.float32)] * 2,
        scratch_shapes=[pltpu.VMEM((out_rows, width), jnp.float32)],
        compiler_params=pltpu.CompilerParams(vmem_limit_bytes=VMEM_LIMIT),
        cost_estimate=pl.CostEstimate(
            flops=6 * out_rows * kept.shape[0] * TILE * width, bytes_accessed=10**7, transcendentals=0
        ),
    )(core.reshape(1), *[in_vmem(v) for v in (high, low, kept, came, own)])


def exchange(value, axes):
    return lax.all_to_all(value, axes, 0, 0, tiled=True)


def gather(value, axes):
    return exchange(jnp.broadcast_to(value, (lax.axis_size(axes),) + value.shape), axes)


def swap(value, axis):
    return lax.ppermute(value, axis, [(0, 1), (1, 0)])


def from_ahead(value, axis, steps):
    size = lax.axis_size(axis)
    return lax.ppermute(value, axis, [(i, (i - steps) % size) for i in range(size)])


def sum_everywhere(mine, other):
    rows, width = mine.shape
    mine = mine + swap(other, "core")
    own = exchange(mine.reshape(-1, rows // lax.axis_size(("x", "zl")), width), ("x", "zl")).sum(0)
    own = gather(own, REP).sum(0)
    mine = gather(own, ("x", "zl")).reshape(rows, width)
    other = swap(mine, "core")
    return jnp.where(
        lax.axis_index("core") == 0, jnp.concatenate([mine, other]), jnp.concatenate([other, mine])
    )


def local(features, weight, cotangent, degree, tile_row, tile_col, edge_dst, edge_src, tile_live):
    own_rows, in_width = features.shape
    hidden_width = weight.shape[1]
    own_blocks = own_rows // TILE
    group_blocks = own_blocks * lax.axis_size(REP)
    half_blocks = own_blocks * lax.axis_size(("x", "zl"))
    blocks = (-1, TILE, hidden_width)
    row_ids = tile_row.reshape(-1)
    live = tile_live.reshape(1)
    slots, edges = edge_dst.shape[2:]
    owner, within = tile_col.reshape(-1) // own_blocks, tile_col.reshape(-1) % own_blocks
    other_core = owner % 2 ^ lax.axis_index("core")
    from_ids = other_core * half_blocks + owner // 2 * own_blocks + within
    x_ahead = (owner // 4 - lax.axis_index("x")) % 4
    other_z = owner // 2 % 2 ^ lax.axis_index("zl")
    to_ids = other_core * half_blocks + (x_ahead * 2 + other_z) * own_blocks + within

    height = -(-in_width // 32) * 32
    scaled, here, scales = project(features.T, weight, degree, height)
    scaled, here, scales = lax.optimization_barrier((scaled, here, scales))
    near = gather(scaled, ("x", "zl"))
    here, near = lax.optimization_barrier((here, near))
    far = swap(near, "core")
    across = swap(here, "zl")
    here_x = [from_ahead(here, "x", steps) for steps in (1, 2, 3)]
    tiles = build_tiles(live, edge_dst.reshape(slots, edges), edge_src.reshape(slots, edges))

    own_source = (lax.axis_index(("x", "zl")) * own_blocks).reshape(1)
    own = jnp.concatenate([(lax.axis_index(REP) * own_blocks).reshape(1), own_source]).astype(jnp.int32)

    def forward(near, far, cotangent, scales):
        sources = [near.reshape(blocks), far.reshape(blocks)]
        (sums,) = aggregate(tiles, live, from_ids, row_ids, own, sources, [group_blocks], False)
        return activate(exchange(sums.reshape(-1, own_rows, hidden_width), REP), cotangent, scales)

    def never(near, far, cotangent, scales):
        return near[0] + cotangent, far[0] - cotangent

    hidden, back_own = lax.cond(live[0] > 0, forward, never, near, far, cotangent, scales)
    across, here_x, back_own = lax.optimization_barrier((across, here_x, back_own))
    across_x = [from_ahead(across, "x", steps) for steps in (1, 2, 3)]
    back_group = lax.cond(
        live[0] > 0,
        lambda back: gather(back, REP),
        lambda back: jnp.broadcast_to(back, (lax.axis_size(REP),) + back.shape),
        back_own,
    )
    across_x, back_group = lax.optimization_barrier((across_x, back_group))
    kept, sent = aggregate(
        tiles, live, row_ids, to_ids, own, [back_group.reshape(blocks)], [half_blocks] * 2, True
    )
    came = swap(sent, "core")
    held = [part for pair in zip([here, *here_x], [across, *across_x]) for part in pair]
    parts = lax.axis_size(BLK)
    out_rows = -(-in_width // (8 * parts)) * 8 * parts
    halves = gradient(split_features(held), lax.axis_index("core"), kept, came, back_own.reshape(blocks), out_rows)
    return (hidden, sum_everywhere(*halves)[:in_width])


def solution(mesh):
    mesh = Mesh(mesh.devices.reshape(4, 2, 2, 4, 2), BLK + REP)
    nodes = P(BLK + REP)
    tile = P(BLK, REP)
    return jax.shard_map(
        local,
        mesh=mesh,
        in_specs=(nodes, P(), nodes, nodes, tile, tile, tile, tile, tile),
        out_specs=(nodes, P()),
        check_vma=False,
    )
```

```python
from functools import partial

import jax
import jax.numpy as jnp
from jax import lax
from jax.experimental import pallas as pl
from jax.experimental.pallas import tpu as pltpu
from jax.sharding import Mesh
from jax.sharding import PartitionSpec as P

TILE = 128
HIGH = lax.Precision.HIGHEST
activation = partial(jax.nn.gelu, approximate=True)
ROWS = 32
PIECE = 3
PARTS = 2
AHEAD = 2
STRIP = 128
UNROLL = 32
VMEM_LIMIT = 28 * 1024 * 1024
BLK = ("x", "zl", "core")
REP = ("y", "zh")


def in_vmem(value):
    return pltpu.with_memory_space_constraint(value, pltpu.VMEM)


def in_hbm(value):
    return pltpu.with_memory_space_constraint(value, pltpu.HBM)


SMEM = pl.BlockSpec(memory_space=pltpu.SMEM)
VMEM = pl.BlockSpec(memory_space=pltpu.VMEM)
ANY = pl.BlockSpec(memory_space=pl.ANY)


def tile_kernel(live_ref, dst_hbm, src_hbm, out_ref, dst_ref, src_ref, tiles, edge_sems, sems):
    live = live_ref[0]
    groups = (live + ROWS - 1) // ROWS
    node_ids = lax.broadcasted_iota(jnp.int32, (TILE, dst_ref.shape[1]), 0).astype(jnp.float32).astype(jnp.bfloat16)
    one, zero = jnp.ones((), jnp.bfloat16), jnp.zeros((), jnp.bfloat16)

    def one_hot(ids):
        hot = ids.astype(jnp.float32).astype(jnp.bfloat16) == node_ids
        return jnp.where(hot, one, zero).astype(jnp.float8_e4m3fn)

    def copies_in(group):
        at = pl.ds(pl.multiple_of(group * ROWS, ROWS), ROWS)
        return [
            pltpu.make_async_copy(dst_hbm.at[at], dst_ref.at[at], edge_sems.at[0, group]),
            pltpu.make_async_copy(src_hbm.at[at], src_ref.at[at], edge_sems.at[1, group]),
        ]

    def start_in(group, carry):
        for copy in copies_in(group):
            copy.start()
        return carry

    def copy_out(group):
        at = pl.ds(pl.multiple_of(group * ROWS, ROWS), ROWS)
        return pltpu.make_async_copy(tiles.at[at], out_ref.at[at], sems.at[group])

    def some_slots(group, carry):
        for copy in copies_in(group):
            copy.wait()
        first = pl.multiple_of(group * ROWS, ROWS)
        dst = dst_ref[pl.ds(first, ROWS)]
        src = src_ref[pl.ds(first, ROWS)]
        for k in range(ROWS):
            dst_ids = jnp.where(first + k < live, dst[k : k + 1], TILE)
            counts = lax.dot_general(
                one_hot(dst_ids),
                one_hot(src[k : k + 1]),
                (((1,), (1,)), ((), ())),
                preferred_element_type=jnp.float32,
            )
            tiles[first + k] = counts.astype(jnp.bfloat16)
        copy_out(group).start()
        return carry

    lax.fori_loop(0, groups, start_in, 0)
    lax.fori_loop(0, groups, some_slots, 0)
    lax.fori_loop(0, groups, lambda group, carry: (copy_out(group).wait(), carry)[1], 0)


def build_tiles(live, edge_dst, edge_src):
    slots, edges = edge_dst.shape
    return pl.pallas_call(
        tile_kernel,
        in_specs=[SMEM, ANY, ANY],
        out_specs=ANY,
        out_shape=pltpu.HBM((slots, TILE, TILE), jnp.bfloat16),
        scratch_shapes=[
            pltpu.VMEM((slots, edges), jnp.int32),
            pltpu.VMEM((slots, edges), jnp.int32),
            pltpu.VMEM((slots, TILE, TILE), jnp.bfloat16),
            pltpu.SemaphoreType.DMA((2, slots // ROWS)),
            pltpu.SemaphoreType.DMA((slots // ROWS,)),
        ],
        compiler_params=pltpu.CompilerParams(vmem_limit_bytes=VMEM_LIMIT),
        cost_estimate=pl.CostEstimate(flops=10**6, bytes_accessed=10**5, transcendentals=0),
    )(live, in_hbm(edge_dst), in_hbm(edge_src))


def aggregate_kernel(parts, targets, transpose, live_ref, pick_ref, place_ref, own_ref, tiles_ref, *refs):
    sources, outs = refs[:parts], refs[parts : parts + targets]
    split, landed, tiles, sems, tile_sems, *more = refs[parts + targets :]
    totals = more[0] if more else outs[0]
    groups = (live_ref[0] + UNROLL - 1) // UNROLL

    def tile_copy(group):
        at = pl.ds(pl.multiple_of(group * UNROLL, UNROLL), UNROLL)
        return pltpu.make_async_copy(tiles_ref.at[at], tiles.at[at], tile_sems.at[group])

    pieces = [
        (p, b) for p, source_ref in enumerate(sources) for b in range(0, source_ref.shape[0], PIECE)
    ]
    copies = []
    for n, (p, b) in enumerate(pieces):
        copy = pltpu.make_async_copy(
            sources[p].at[pl.ds(b, PIECE)], landed.at[pl.ds(n * PIECE, PIECE)], sems.at[n]
        )
        copy.start()
        copies.append(copy)
    for group in range(AHEAD):
        pl.when(group < groups)(tile_copy(group).start)
    totals[...] = jnp.zeros_like(totals)

    for n, copy in enumerate(copies):
        copy.wait()
        if not transpose:

            @pl.when(own_ref[1] == n * PIECE)
            def _():
                totals[pl.ds(own_ref[0], PIECE)] = landed[n * PIECE : (n + 1) * PIECE]

        def split_block(k, carry):
            value = landed[n * PIECE + k]
            high = value.astype(jnp.bfloat16)
            split[n * PIECE + k, :TILE] = high
            split[n * PIECE + k, TILE:] = (value - high.astype(jnp.float32)).astype(jnp.bfloat16)
            return carry

        lax.fori_loop(0, PIECE, split_block, 0)

    def some_tiles(group, carry):
        tile_copy(group).wait()
        pl.when(group + AHEAD < groups)(lambda: tile_copy(group + AHEAD).start())
        first = group * UNROLL
        products = []
        for k in range(UNROLL):
            tile = tiles[first + k]
            picked = split[pick_ref[first + k]]
            twice = jnp.concatenate([tile, tile], axis=0 if transpose else 1)
            products.append(
                lax.dot_general(
                    twice,
                    picked,
                    (((0 if transpose else 1,), (0,)), ((), ())),
                    preferred_element_type=jnp.float32,
                )
            )
        for k in range(UNROLL):
            totals[place_ref[first + k]] += products[k]
        return carry

    lax.fori_loop(0, groups, some_tiles, 0)
    if more:
        for p, out_ref in enumerate(outs):
            count = out_ref.shape[0]
            out_ref[...] = totals[p * count : (p + 1) * count]


def aggregate(tiles, live, pick_ids, place_ids, own, sources, target_blocks, transpose):
    slots = tiles.shape[0]
    source_blocks, _, width = sources[0].shape
    parts, targets = len(sources), len(target_blocks)
    return pl.pallas_call(
        partial(aggregate_kernel, parts, targets, transpose),
        in_specs=[SMEM] * 4 + [ANY] * (1 + parts),
        out_specs=[VMEM] * targets,
        out_shape=[pltpu.VMEM((b, TILE, width), jnp.float32) for b in target_blocks],
        scratch_shapes=[
            pltpu.VMEM((parts * source_blocks, 2 * TILE, width), jnp.bfloat16),
            pltpu.VMEM((parts * source_blocks, TILE, width), jnp.float32),
            pltpu.VMEM(tiles.shape, jnp.bfloat16),
            pltpu.SemaphoreType.DMA((parts * source_blocks // PIECE,)),
            pltpu.SemaphoreType.DMA((slots // UNROLL,)),
        ]
        + [pltpu.VMEM((sum(target_blocks), TILE, width), jnp.float32)] * (targets > 1),
        compiler_params=pltpu.CompilerParams(vmem_limit_bytes=VMEM_LIMIT),
        cost_estimate=pl.CostEstimate(
            flops=10**6, bytes_accessed=10**5, transcendentals=0
        ),
    )(live, pick_ids, place_ids, own, in_hbm(tiles), *sources)


def activate_kernel(parts_ref, cotangent_ref, scales_ref, hidden_ref, back_ref):
    scales = jnp.concatenate([scales_ref[...]] * (hidden_ref.shape[1] // TILE), axis=1)
    pre = parts_ref[...].sum(0) * scales
    hidden, pull = jax.vjp(activation, pre)
    hidden_ref[...] = hidden
    back_ref[...] = pull(cotangent_ref[...])[0] * scales


def activate(parts, cotangent, scales):
    count, rows, width = parts.shape
    block = pl.BlockSpec((STRIP, width), lambda g: (g, 0))
    return pl.pallas_call(
        activate_kernel,
        grid=(rows // STRIP,),
        in_specs=[
            pl.BlockSpec((count, STRIP, width), lambda g: (0, g, 0)),
            block,
            pl.BlockSpec((STRIP, TILE), lambda g: (g, 0)),
        ],
        out_specs=[block, block],
        out_shape=[jax.ShapeDtypeStruct((rows, width), jnp.float32)] * 2,
        compiler_params=pltpu.CompilerParams(vmem_limit_bytes=VMEM_LIMIT),
    )(parts, cotangent, scales)


def project_kernel(
    features_hbm,
    weight_hbm,
    degree_hbm,
    scaled_ref,
    turned_ref,
    scales_ref,
    features_ref,
    weight_ref,
    degree_ref,
    padded,
    sems,
):
    height, in_width = turned_ref.shape[0], features_ref.shape[0]
    features_in = pltpu.make_async_copy(features_hbm, features_ref, sems.at[0])
    weight_in = pltpu.make_async_copy(weight_hbm, weight_ref, sems.at[1])
    degree_in = pltpu.make_async_copy(degree_hbm, degree_ref, sems.at[2])
    degree_in.start()
    features_in.start()
    weight_in.start()
    degree_in.wait()
    scales = lax.rsqrt(degree_ref[...].astype(jnp.float32)).reshape(1, -1)
    features_in.wait()
    turned_ref[:in_width] = features_ref[...] * scales
    turned_ref[in_width:] = jnp.zeros((height - in_width, turned_ref.shape[1]), jnp.float32)
    weight_in.wait()
    padded[:in_width] = weight_ref[...]
    padded[in_width:] = jnp.zeros((height - in_width, padded.shape[1]), jnp.float32)
    scaled_ref[...] = lax.dot_general(
        turned_ref[...],
        padded[...],
        (((0,), (0,)), ((), ())),
        precision=HIGH,
        preferred_element_type=jnp.float32,
    )
    scales_ref[...] = jnp.broadcast_to(scales, (TILE, scales.shape[1])).T


def two_terms(value):
    high = value.astype(jnp.bfloat16)
    return high, (value - high.astype(jnp.float32)).astype(jnp.bfloat16)


def project(features, weight, degree, height):
    in_width, rows = features.shape
    width = weight.shape[1]
    return pl.pallas_call(
        project_kernel,
        in_specs=[ANY] * 3,
        out_specs=[VMEM] * 3,
        out_shape=[
            jax.ShapeDtypeStruct((rows, width), jnp.float32),
            jax.ShapeDtypeStruct((height, rows), jnp.float32),
            jax.ShapeDtypeStruct((rows, TILE), jnp.float32),
        ],
        scratch_shapes=[
            pltpu.VMEM(features.shape, jnp.float32),
            pltpu.VMEM(weight.shape, jnp.float32),
            pltpu.VMEM(degree.shape, jnp.int32),
            pltpu.VMEM((height, width), jnp.float32),
            pltpu.SemaphoreType.DMA((3,)),
        ],
        compiler_params=pltpu.CompilerParams(vmem_limit_bytes=VMEM_LIMIT),
    )(in_hbm(features), in_hbm(weight), in_hbm(degree))


def split_features_kernel(*refs):
    features, (high_ref, low_ref) = refs[:-2], refs[-2:]
    nodes = features[0].shape[1]
    for p, part_ref in enumerate(features):
        at = pl.ds(p % PARTS * nodes, nodes)
        high, low = two_terms(part_ref[...])
        high_ref[p // PARTS, :, at] = high
        low_ref[p // PARTS, :, at] = low


def split_features(features):
    height, nodes = features[0].shape
    shape = (len(features) // PARTS, height, PARTS * nodes)
    return pl.pallas_call(
        split_features_kernel,
        in_specs=[VMEM] * len(features),
        out_specs=[VMEM] * 2,
        out_shape=[pltpu.VMEM(shape, jnp.bfloat16)] * 2,
        compiler_params=pltpu.CompilerParams(vmem_limit_bytes=VMEM_LIMIT),
        cost_estimate=pl.CostEstimate(flops=10**6, bytes_accessed=10**7, transcendentals=0),
    )(*[in_vmem(f) for f in features])


def gradient_kernel(core_ref, high_ref, low_ref, kept_ref, came_ref, own_ref, mine_ref, other_ref, out_ref):
    parts, height, nodes = high_ref.shape
    blocks = nodes // TILE
    out_ref[...] = jnp.zeros_like(out_ref)
    for p in range(parts):
        rows = kept_ref[p * blocks : (p + 1) * blocks] + came_ref[p * blocks : (p + 1) * blocks]
        if p == 0:
            own = own_ref.shape[0]
            rows = jnp.concatenate([rows[:own] + own_ref[...], rows[own:]])
        rows = rows.reshape(nodes, out_ref.shape[1])
        rows_high, rows_low = two_terms(rows)
        right = jnp.concatenate([rows_high, rows_low, rows_high], axis=0)
        left = jnp.concatenate([high_ref[p], high_ref[p], low_ref[p]], axis=1)
        out_ref[:height] += jnp.dot(left, right, preferred_element_type=jnp.float32)
    half = mine_ref.shape[0]
    mine_ref[...] = out_ref[pl.ds(pl.multiple_of(core_ref[0] * half, half), half)]
    other_ref[...] = out_ref[pl.ds(pl.multiple_of((1 - core_ref[0]) * half, half), half)]


def gradient(features, core, kept, came, own, out_rows):
    high, low = features
    width = kept.shape[2]
    return pl.pallas_call(
        gradient_kernel,
        in_specs=[SMEM] + [VMEM] * 5,
        out_specs=[VMEM] * 2,
        out_shape=[pltpu.VMEM((out_rows // 2, width), jnp.float32)] * 2,
        scratch_shapes=[pltpu.VMEM((out_rows, width), jnp.float32)],
        compiler_params=pltpu.CompilerParams(vmem_limit_bytes=VMEM_LIMIT),
        cost_estimate=pl.CostEstimate(
            flops=6 * out_rows * kept.shape[0] * TILE * width, bytes_accessed=10**7, transcendentals=0
        ),
    )(core.reshape(1), *[in_vmem(v) for v in (high, low, kept, came, own)])


def exchange(value, axes):
    return lax.all_to_all(value, axes, 0, 0, tiled=True)


def gather(value, axes):
    return exchange(jnp.broadcast_to(value, (lax.axis_size(axes),) + value.shape), axes)


def swap(value, axis):
    return lax.ppermute(value, axis, [(0, 1), (1, 0)])


def from_ahead(value, axis, steps):
    size = lax.axis_size(axis)
    return lax.ppermute(value, axis, [(i, (i - steps) % size) for i in range(size)])


def sum_everywhere(mine, other):
    rows, width = mine.shape
    mine = mine + swap(other, "core")
    own = exchange(mine.reshape(-1, rows // lax.axis_size(("x", "zl")), width), ("x", "zl")).sum(0)
    own = gather(own, REP).sum(0)
    mine = gather(own, ("x", "zl")).reshape(rows, width)
    other = swap(mine, "core")
    return jnp.where(
        lax.axis_index("core") == 0, jnp.concatenate([mine, other]), jnp.concatenate([other, mine])
    )


def local(features, weight, cotangent, degree, tile_row, tile_col, edge_dst, edge_src, tile_live):
    own_rows, in_width = features.shape
    hidden_width = weight.shape[1]
    own_blocks = own_rows // TILE
    group_blocks = own_blocks * lax.axis_size(REP)
    half_blocks = own_blocks * lax.axis_size(("x", "zl"))
    blocks = (-1, TILE, hidden_width)
    row_ids = tile_row.reshape(-1)
    live = tile_live.reshape(1)
    always = live[0] >= 0
    slots, edges = edge_dst.shape[2:]
    owner, within = tile_col.reshape(-1) // own_blocks, tile_col.reshape(-1) % own_blocks
    other_core = owner % 2 ^ lax.axis_index("core")
    from_ids = other_core * half_blocks + owner // 2 * own_blocks + within
    x_ahead = (owner // 4 - lax.axis_index("x")) % 4
    other_z = owner // 2 % 2 ^ lax.axis_index("zl")
    to_ids = other_core * half_blocks + (x_ahead * 2 + other_z) * own_blocks + within

    height = -(-in_width // 32) * 32
    scaled, here, scales = project(features.T, weight, degree, height)
    scaled, here, scales = lax.optimization_barrier((scaled, here, scales))
    near = gather(scaled, ("x", "zl"))
    here, near = lax.optimization_barrier((here, near))
    far = swap(near, "core")
    across = swap(here, "zl")
    here_x = [from_ahead(here, "x", steps) for steps in (1, 2, 3)]
    tiles = build_tiles(live, edge_dst.reshape(slots, edges), edge_src.reshape(slots, edges))

    own_source = (lax.axis_index(("x", "zl")) * own_blocks).reshape(1)
    own = jnp.concatenate([(lax.axis_index(REP) * own_blocks).reshape(1), own_source]).astype(jnp.int32)

    def forward(near, far, cotangent, scales):
        sources = [near.reshape(blocks), far.reshape(blocks)]
        (sums,) = aggregate(tiles, live, from_ids, row_ids, own, sources, [group_blocks], False)
        return activate(exchange(sums.reshape(-1, own_rows, hidden_width), REP), cotangent, scales)

    def never(near, far, cotangent, scales):
        return near[0] + cotangent, far[0] - cotangent

    hidden, back_own = lax.cond(always, forward, never, near, far, cotangent, scales)
    across, here_x, back_own = lax.optimization_barrier((across, here_x, back_own))
    across_x = [from_ahead(across, "x", steps) for steps in (1, 2, 3)]
    back_group = lax.cond(
        always,
        lambda back: gather(back, REP),
        lambda back: jnp.broadcast_to(back, (lax.axis_size(REP),) + back.shape),
        back_own,
    )
    across_x, back_group = lax.optimization_barrier((across_x, back_group))
    kept, sent = aggregate(
        tiles, live, row_ids, to_ids, own, [back_group.reshape(blocks)], [half_blocks] * 2, True
    )
    came = swap(sent, "core")
    held = [part for pair in zip([here, *here_x], [across, *across_x]) for part in pair]
    parts = lax.axis_size(BLK)
    out_rows = -(-in_width // (8 * parts)) * 8 * parts
    halves = gradient(split_features(held), lax.axis_index("core"), kept, came, back_own.reshape(blocks), out_rows)
    return (hidden, sum_everywhere(*halves)[:in_width])


def solution(mesh):
    mesh = Mesh(mesh.devices.reshape(4, 2, 2, 4, 2), BLK + REP)
    nodes = P(BLK + REP)
    tile = P(BLK, REP)
    return jax.shard_map(
        local,
        mesh=mesh,
        in_specs=(nodes, P(), nodes, nodes, tile, tile, tile, tile, tile),
        out_specs=(nodes, P()),
        check_vma=False,
    )
```

```python
from functools import partial

import jax
import jax.numpy as jnp
from jax import lax
from jax.experimental import pallas as pl
from jax.experimental.pallas import tpu as pltpu
from jax.sharding import Mesh
from jax.sharding import PartitionSpec as P

TILE = 128
HIGH = lax.Precision.HIGHEST
activation = partial(jax.nn.gelu, approximate=True)
ROWS = 32
PIECE = 3
PARTS = 2
AHEAD = 2
STRIP = 128
UNROLL = 32
VMEM_LIMIT = 28 * 1024 * 1024
BLK = ("x", "zl", "core")
REP = ("y", "zh")


def in_vmem(value):
    return pltpu.with_memory_space_constraint(value, pltpu.VMEM)


def in_hbm(value):
    return pltpu.with_memory_space_constraint(value, pltpu.HBM)


SMEM = pl.BlockSpec(memory_space=pltpu.SMEM)
VMEM = pl.BlockSpec(memory_space=pltpu.VMEM)
ANY = pl.BlockSpec(memory_space=pl.ANY)


def tile_kernel(live_ref, dst_hbm, src_hbm, out_ref, dst_ref, src_ref, tiles, edge_sems, sems):
    live = live_ref[0]
    groups = (live + ROWS - 1) // ROWS
    node_ids = lax.broadcasted_iota(jnp.int32, (TILE, dst_ref.shape[1]), 0).astype(jnp.float32).astype(jnp.bfloat16)
    one, zero = jnp.ones((), jnp.bfloat16), jnp.zeros((), jnp.bfloat16)

    def one_hot(ids):
        hot = ids.astype(jnp.float32).astype(jnp.bfloat16) == node_ids
        return jnp.where(hot, one, zero).astype(jnp.float8_e4m3fn)

    def copies_in(group):
        at = pl.ds(pl.multiple_of(group * ROWS, ROWS), ROWS)
        return [
            pltpu.make_async_copy(dst_hbm.at[at], dst_ref.at[at], edge_sems.at[0, group]),
            pltpu.make_async_copy(src_hbm.at[at], src_ref.at[at], edge_sems.at[1, group]),
        ]

    def start_in(group, carry):
        for copy in copies_in(group):
            copy.start()
        return carry

    def copy_out(group):
        at = pl.ds(pl.multiple_of(group * ROWS, ROWS), ROWS)
        return pltpu.make_async_copy(tiles.at[at], out_ref.at[at], sems.at[group])

    def some_slots(group, carry):
        for copy in copies_in(group):
            copy.wait()
        first = pl.multiple_of(group * ROWS, ROWS)
        dst = dst_ref[pl.ds(first, ROWS)]
        src = src_ref[pl.ds(first, ROWS)]
        for k in range(ROWS):
            dst_ids = jnp.where(first + k < live, dst[k : k + 1], TILE)
            counts = lax.dot_general(
                one_hot(dst_ids),
                one_hot(src[k : k + 1]),
                (((1,), (1,)), ((), ())),
                preferred_element_type=jnp.float32,
            )
            tiles[first + k] = counts.astype(jnp.bfloat16)
        copy_out(group).start()
        return carry

    lax.fori_loop(0, groups, start_in, 0)
    lax.fori_loop(0, groups, some_slots, 0)
    lax.fori_loop(0, groups, lambda group, carry: (copy_out(group).wait(), carry)[1], 0)


def build_tiles(live, edge_dst, edge_src):
    slots, edges = edge_dst.shape
    return pl.pallas_call(
        tile_kernel,
        in_specs=[SMEM, ANY, ANY],
        out_specs=ANY,
        out_shape=pltpu.HBM((slots, TILE, TILE), jnp.bfloat16),
        scratch_shapes=[
            pltpu.VMEM((slots, edges), jnp.int32),
            pltpu.VMEM((slots, edges), jnp.int32),
            pltpu.VMEM((slots, TILE, TILE), jnp.bfloat16),
            pltpu.SemaphoreType.DMA((2, slots // ROWS)),
            pltpu.SemaphoreType.DMA((slots // ROWS,)),
        ],
        compiler_params=pltpu.CompilerParams(vmem_limit_bytes=VMEM_LIMIT),
        cost_estimate=pl.CostEstimate(flops=10**6, bytes_accessed=10**5, transcendentals=0),
    )(live, in_hbm(edge_dst), in_hbm(edge_src))


def aggregate_kernel(parts, targets, transpose, live_ref, pick_ref, place_ref, own_ref, tiles_ref, *refs):
    sources, outs = refs[:parts], refs[parts : parts + targets]
    split, landed, tiles, sems, tile_sems, *more = refs[parts + targets :]
    totals = more[0] if more else outs[0]
    groups = (live_ref[0] + UNROLL - 1) // UNROLL

    def tile_copy(group):
        at = pl.ds(pl.multiple_of(group * UNROLL, UNROLL), UNROLL)
        return pltpu.make_async_copy(tiles_ref.at[at], tiles.at[at], tile_sems.at[group])

    pieces = [
        (p, b) for p, source_ref in enumerate(sources) for b in range(0, source_ref.shape[0], PIECE)
    ]
    copies = []
    for n, (p, b) in enumerate(pieces):
        copy = pltpu.make_async_copy(
            sources[p].at[pl.ds(b, PIECE)], landed.at[pl.ds(n * PIECE, PIECE)], sems.at[n]
        )
        copy.start()
        copies.append(copy)
    for group in range(AHEAD):
        pl.when(group < groups)(tile_copy(group).start)
    totals[...] = jnp.zeros_like(totals)

    for n, copy in enumerate(copies):
        copy.wait()
        if not transpose:

            @pl.when(own_ref[1] == n * PIECE)
            def _():
                totals[pl.ds(own_ref[0], PIECE)] = landed[n * PIECE : (n + 1) * PIECE]

        def split_block(k, carry):
            value = landed[n * PIECE + k]
            high = value.astype(jnp.bfloat16)
            split[n * PIECE + k, :TILE] = high
            split[n * PIECE + k, TILE:] = (value - high.astype(jnp.float32)).astype(jnp.bfloat16)
            return carry

        lax.fori_loop(0, PIECE, split_block, 0)

    def some_tiles(group, carry):
        tile_copy(group).wait()
        pl.when(group + AHEAD < groups)(lambda: tile_copy(group + AHEAD).start())
        first = group * UNROLL
        products = []
        for k in range(UNROLL):
            tile = tiles[first + k]
            picked = split[pick_ref[first + k]]
            twice = jnp.concatenate([tile, tile], axis=0 if transpose else 1)
            products.append(
                lax.dot_general(
                    twice,
                    picked,
                    (((0 if transpose else 1,), (0,)), ((), ())),
                    preferred_element_type=jnp.float32,
                )
            )
        for k in range(UNROLL):
            totals[place_ref[first + k]] += products[k]
        return carry

    lax.fori_loop(0, groups, some_tiles, 0)
    if more:
        for p, out_ref in enumerate(outs):
            count = out_ref.shape[0]
            out_ref[...] = totals[p * count : (p + 1) * count]


def aggregate(tiles, live, pick_ids, place_ids, own, sources, target_blocks, transpose):
    slots = tiles.shape[0]
    source_blocks, _, width = sources[0].shape
    parts, targets = len(sources), len(target_blocks)
    return pl.pallas_call(
        partial(aggregate_kernel, parts, targets, transpose),
        in_specs=[SMEM] * 4 + [ANY] * (1 + parts),
        out_specs=[VMEM] * targets,
        out_shape=[pltpu.VMEM((b, TILE, width), jnp.float32) for b in target_blocks],
        scratch_shapes=[
            pltpu.VMEM((parts * source_blocks, 2 * TILE, width), jnp.bfloat16),
            pltpu.VMEM((parts * source_blocks, TILE, width), jnp.float32),
            pltpu.VMEM(tiles.shape, jnp.bfloat16),
            pltpu.SemaphoreType.DMA((parts * source_blocks // PIECE,)),
            pltpu.SemaphoreType.DMA((slots // UNROLL,)),
        ]
        + [pltpu.VMEM((sum(target_blocks), TILE, width), jnp.float32)] * (targets > 1),
        compiler_params=pltpu.CompilerParams(vmem_limit_bytes=VMEM_LIMIT),
        cost_estimate=pl.CostEstimate(
            flops=10**6, bytes_accessed=10**5, transcendentals=0
        ),
    )(live, pick_ids, place_ids, own, in_hbm(tiles), *sources)


def activate_kernel(parts_ref, cotangent_ref, scales_ref, hidden_ref, back_ref):
    scales = jnp.concatenate([scales_ref[...]] * (hidden_ref.shape[1] // TILE), axis=1)
    pre = parts_ref[...].sum(0) * scales
    hidden, pull = jax.vjp(activation, pre)
    hidden_ref[...] = hidden
    back_ref[...] = pull(cotangent_ref[...])[0] * scales


def activate(parts, cotangent, scales):
    count, rows, width = parts.shape
    block = pl.BlockSpec((STRIP, width), lambda g: (g, 0))
    return pl.pallas_call(
        activate_kernel,
        grid=(rows // STRIP,),
        in_specs=[
            pl.BlockSpec((count, STRIP, width), lambda g: (0, g, 0)),
            block,
            pl.BlockSpec((STRIP, TILE), lambda g: (g, 0)),
        ],
        out_specs=[block, block],
        out_shape=[jax.ShapeDtypeStruct((rows, width), jnp.float32)] * 2,
        compiler_params=pltpu.CompilerParams(vmem_limit_bytes=VMEM_LIMIT),
    )(parts, cotangent, scales)


def project_kernel(
    features_hbm,
    weight_hbm,
    degree_hbm,
    scaled_ref,
    turned_ref,
    scales_ref,
    features_ref,
    weight_ref,
    degree_ref,
    padded,
    sems,
):
    height, in_width = turned_ref.shape[0], features_ref.shape[0]
    features_in = pltpu.make_async_copy(features_hbm, features_ref, sems.at[0])
    weight_in = pltpu.make_async_copy(weight_hbm, weight_ref, sems.at[1])
    degree_in = pltpu.make_async_copy(degree_hbm, degree_ref, sems.at[2])
    degree_in.start()
    features_in.start()
    weight_in.start()
    degree_in.wait()
    scales = lax.rsqrt(degree_ref[...].astype(jnp.float32)).reshape(1, -1)
    features_in.wait()
    turned_ref[:in_width] = features_ref[...] * scales
    turned_ref[in_width:] = jnp.zeros((height - in_width, turned_ref.shape[1]), jnp.float32)
    weight_in.wait()
    padded[:in_width] = weight_ref[...]
    padded[in_width:] = jnp.zeros((height - in_width, padded.shape[1]), jnp.float32)
    scaled_ref[...] = lax.dot_general(
        turned_ref[...],
        padded[...],
        (((0,), (0,)), ((), ())),
        precision=HIGH,
        preferred_element_type=jnp.float32,
    )
    scales_ref[...] = jnp.broadcast_to(scales, (TILE, scales.shape[1])).T


def two_terms(value):
    high = value.astype(jnp.bfloat16)
    return high, (value - high.astype(jnp.float32)).astype(jnp.bfloat16)


def project(features, weight, degree, height):
    in_width, rows = features.shape
    width = weight.shape[1]
    return pl.pallas_call(
        project_kernel,
        in_specs=[ANY] * 3,
        out_specs=[VMEM] * 3,
        out_shape=[
            jax.ShapeDtypeStruct((rows, width), jnp.float32),
            jax.ShapeDtypeStruct((height, rows), jnp.float32),
            jax.ShapeDtypeStruct((rows, TILE), jnp.float32),
        ],
        scratch_shapes=[
            pltpu.VMEM(features.shape, jnp.float32),
            pltpu.VMEM(weight.shape, jnp.float32),
            pltpu.VMEM(degree.shape, jnp.int32),
            pltpu.VMEM((height, width), jnp.float32),
            pltpu.SemaphoreType.DMA((3,)),
        ],
        compiler_params=pltpu.CompilerParams(vmem_limit_bytes=VMEM_LIMIT),
    )(in_hbm(features), in_hbm(weight), in_hbm(degree))


def split_features_kernel(*refs):
    features, (high_ref, low_ref) = refs[:-2], refs[-2:]
    nodes = features[0].shape[1]
    for p, part_ref in enumerate(features):
        at = pl.ds(p % PARTS * nodes, nodes)
        high, low = two_terms(part_ref[...])
        high_ref[p // PARTS, :, at] = high
        low_ref[p // PARTS, :, at] = low


def split_features(features):
    height, nodes = features[0].shape
    shape = (len(features) // PARTS, height, PARTS * nodes)
    return pl.pallas_call(
        split_features_kernel,
        in_specs=[VMEM] * len(features),
        out_specs=[VMEM] * 2,
        out_shape=[pltpu.VMEM(shape, jnp.bfloat16)] * 2,
        compiler_params=pltpu.CompilerParams(vmem_limit_bytes=VMEM_LIMIT),
        cost_estimate=pl.CostEstimate(flops=10**6, bytes_accessed=10**7, transcendentals=0),
    )(*[in_vmem(f) for f in features])


def gradient_kernel(core_ref, high_ref, low_ref, kept_ref, came_ref, own_ref, mine_ref, other_ref, out_ref):
    parts, height, nodes = high_ref.shape
    blocks = nodes // TILE
    out_ref[...] = jnp.zeros_like(out_ref)
    for p in range(parts):
        rows = kept_ref[p * blocks : (p + 1) * blocks] + came_ref[p * blocks : (p + 1) * blocks]
        if p == 0:
            own = own_ref.shape[0]
            rows = jnp.concatenate([rows[:own] + own_ref[...], rows[own:]])
        rows = rows.reshape(nodes, out_ref.shape[1])
        rows_high, rows_low = two_terms(rows)
        right = jnp.concatenate([rows_high, rows_low, rows_high], axis=0)
        left = jnp.concatenate([high_ref[p], high_ref[p], low_ref[p]], axis=1)
        out_ref[:height] += jnp.dot(left, right, preferred_element_type=jnp.float32)
    half = mine_ref.shape[0]
    mine_ref[...] = out_ref[pl.ds(pl.multiple_of(core_ref[0] * half, half), half)]
    other_ref[...] = out_ref[pl.ds(pl.multiple_of((1 - core_ref[0]) * half, half), half)]


def gradient(features, core, kept, came, own, out_rows):
    high, low = features
    width = kept.shape[2]
    return pl.pallas_call(
        gradient_kernel,
        in_specs=[SMEM] + [VMEM] * 5,
        out_specs=[VMEM] * 2,
        out_shape=[pltpu.VMEM((out_rows // 2, width), jnp.float32)] * 2,
        scratch_shapes=[pltpu.VMEM((out_rows, width), jnp.float32)],
        compiler_params=pltpu.CompilerParams(vmem_limit_bytes=VMEM_LIMIT),
        cost_estimate=pl.CostEstimate(
            flops=6 * out_rows * kept.shape[0] * TILE * width, bytes_accessed=10**7, transcendentals=0
        ),
    )(core.reshape(1), *[in_vmem(v) for v in (high, low, kept, came, own)])


def exchange(value, axes):
    return lax.all_to_all(value, axes, 0, 0, tiled=True)


def gather(value, axes):
    return exchange(jnp.broadcast_to(value, (lax.axis_size(axes),) + value.shape), axes)


def swap(value, axis):
    return lax.ppermute(value, axis, [(0, 1), (1, 0)])


def from_ahead(value, axis, steps):
    size = lax.axis_size(axis)
    return lax.ppermute(value, axis, [(i, (i - steps) % size) for i in range(size)])


def sum_everywhere(mine, other):
    rows, width = mine.shape
    mine = mine + swap(other, "core")
    own = exchange(mine.reshape(-1, rows // lax.axis_size(("x", "zl")), width), ("x", "zl")).sum(0)
    own = gather(own, REP).sum(0)
    mine = gather(own, ("x", "zl")).reshape(rows, width)
    other = swap(mine, "core")
    return jnp.where(
        lax.axis_index("core") == 0, jnp.concatenate([mine, other]), jnp.concatenate([other, mine])
    )


def local(features, weight, cotangent, degree, tile_row, tile_col, edge_dst, edge_src, tile_live):
    own_rows, in_width = features.shape
    hidden_width = weight.shape[1]
    own_blocks = own_rows // TILE
    group_blocks = own_blocks * lax.axis_size(REP)
    half_blocks = own_blocks * lax.axis_size(("x", "zl"))
    blocks = (-1, TILE, hidden_width)
    row_ids = tile_row.reshape(-1)
    live = tile_live.reshape(1)
    always = live[0] >= 0
    slots, edges = edge_dst.shape[2:]
    owner, within = tile_col.reshape(-1) // own_blocks, tile_col.reshape(-1) % own_blocks
    other_core = owner % 2 ^ lax.axis_index("core")
    from_ids = other_core * half_blocks + owner // 2 * own_blocks + within
    x_ahead = (owner // 4 - lax.axis_index("x")) % 4
    other_z = owner // 2 % 2 ^ lax.axis_index("zl")
    to_ids = other_core * half_blocks + (x_ahead * 2 + other_z) * own_blocks + within

    height = -(-in_width // 32) * 32
    scaled, here, scales = project(features.T, weight, degree, height)
    scaled, here, scales = lax.optimization_barrier((scaled, here, scales))
    near = gather(scaled, ("x", "zl"))
    here, near = lax.optimization_barrier((here, near))
    far = swap(near, "core")
    across = swap(here, "zl")
    here_x = [from_ahead(here, "x", steps) for steps in (1, 2, 3)]
    tiles = build_tiles(live, edge_dst.reshape(slots, edges), edge_src.reshape(slots, edges))

    own_source = (lax.axis_index(("x", "zl")) * own_blocks).reshape(1)
    own = jnp.concatenate([(lax.axis_index(REP) * own_blocks).reshape(1), own_source]).astype(jnp.int32)

    def forward(near, far, cotangent, scales):
        sources = [near.reshape(blocks), far.reshape(blocks)]
        (sums,) = aggregate(tiles, live, from_ids, row_ids, own, sources, [group_blocks], False)
        return activate(exchange(sums.reshape(-1, own_rows, hidden_width), REP), cotangent, scales)

    def never(near, far, cotangent, scales):
        return near[0] + far[0], near[0] - far[0]

    hidden, back_own = lax.cond(always, forward, never, near, far, cotangent, scales)
    across, here_x, back_own = lax.optimization_barrier((across, here_x, back_own))
    across_x = [from_ahead(across, "x", steps) for steps in (1, 2, 3)]
    back_group = lax.cond(
        always,
        lambda back: gather(back, REP),
        lambda back: jnp.broadcast_to(back, (lax.axis_size(REP),) + back.shape),
        back_own,
    )
    across_x, back_group = lax.optimization_barrier((across_x, back_group))
    kept, sent = aggregate(
        tiles, live, row_ids, to_ids, own, [back_group.reshape(blocks)], [half_blocks] * 2, True
    )
    came = swap(sent, "core")
    held = [part for pair in zip([here, *here_x], [across, *across_x]) for part in pair]
    parts = lax.axis_size(BLK)
    out_rows = -(-in_width // (8 * parts)) * 8 * parts
    halves = gradient(split_features(held), lax.axis_index("core"), kept, came, back_own.reshape(blocks), out_rows)
    return (hidden, sum_everywhere(*halves)[:in_width])


def solution(mesh):
    mesh = Mesh(mesh.devices.reshape(4, 2, 2, 4, 2), BLK + REP)
    nodes = P(BLK + REP)
    tile = P(BLK, REP)
    return jax.shard_map(
        local,
        mesh=mesh,
        in_specs=(nodes, P(), nodes, nodes, tile, tile, tile, tile, tile),
        out_specs=(nodes, P()),
        check_vma=False,
    )
```
